32 devices in a mesh: elem: 8 (over z, x), plane: 4 (over y, core).
Axes of the slice: x: 2, y: 2, z: 4, core: 2. Of those that a mesh axis runs over, the one named last changes fastest.
Arguments:
- velocity: float32 [3, 64, 81, 256], P(None, 'plane', None, 'elem'), may hold values from -4.5 to 4.5
- geometry: float32 [4, 100, 256], P(None, None, 'elem'), may hold values from -3 to 3
- jacobian: float32 [100, 256], P(None, 'elem'), may hold values from 0.5 to 2
- frame_flip: int32 [8], P('elem'), may hold values from 0 to 1
Outputs:
- advection: float32 [3, 64, 81, 256], P(None, 'plane', None, 'elem')
- svv_force: float32 [3, 64, 81, 256], P(None, 'plane', None, 'elem')
The draws below stay inside these ranges and needn't reach their ends.
All inputs are finite; a program needn't handle non-finite values.
Results may differ from the reference program's by a relative error of at most 0.00005.
Values sent between devices are 32-bit elements; how exact they have to be, the bound alone decides.
A program may use at most 64 MiB of HBM per device.

```python
import math
import jax
import jax.numpy as jnp
import numpy as np
from jax import lax

P_SIZE = 8
Q = 10
NZ = 64
EY = 8
EX = 4
E_ALL = 256
N_ELEM = 8


def draw_velocity(key, part):
    key = jax.random.fold_in(key, 17)
    noise_key, smooth_key, rough_key = jax.random.split(key, 3)
    full_shape = (3, NZ, (P_SIZE + 1) * (P_SIZE + 1), E_ALL)
    fluctuation = jax.random.truncated_normal(noise_key, -3.0, 3.0, full_shape, jnp.float32)
    smooth = jnp.exp(jax.random.uniform(smooth_key, (E_ALL,), jnp.float32, jnp.log(0.2), jnp.log(1.0)))
    roughness = jax.random.uniform(rough_key, full_shape, jnp.float32, 0.5, 1.5)
    degrees = jnp.maximum(jnp.arange(P_SIZE + 1), 1).astype(jnp.float32)
    highest = jnp.maximum(degrees[:, None], degrees[None, :]).reshape(-1)
    band_level = (jnp.arange(NZ) // 2).astype(jnp.float32) / (NZ // 2)
    tail_modes = highest > 4.0
    envelope = jnp.exp(-1.2 * band_level)[:, None, None] * jnp.exp(-0.35 * smooth[None, None, :] * highest[None, :, None])
    envelope = envelope * jnp.where(tail_modes[None, :, None], jnp.exp(0.9 * band_level)[:, None, None], 1.0)
    return fluctuation * roughness * envelope[None]


def place_ends(values, rng, least, high):
    place = [jax.random.randint(jax.random.fold_in(rng, axis), (), 0, length) for axis, length in enumerate(values.shape)]
    widest = values.shape.index(max(values.shape))
    beside = place[:widest] + [(place[widest] + 1) % values.shape[widest]] + place[widest + 1:]
    return values.at[tuple(place)].set(least).at[tuple(beside)].set(high)


def shard_levels(own_key, dims, cuts, smallest, top_value):
    loudness = 1.0
    for dim, blocks in cuts:
        draws = jax.random.uniform(jax.random.fold_in(jax.random.fold_in(own_key, 6), dim), (blocks,), jnp.float32, smallest / len(cuts), top_value / len(cuts))
        loudness = loudness * jnp.repeat(jnp.exp(draws), dims[dim] // blocks).reshape((-1,) + (1,) * (len(dims) - 1 - dim))
    return loudness


def scatter_about(rng, dims, spread, reach, cuts=(), dtype=jnp.bfloat16):
    entries = jax.random.normal(rng, dims, jnp.float32) * spread
    if len(cuts) > 0:
        entries = shard_levels(rng, dims, cuts, -0.22, 0.18) * entries
    return jnp.clip(entries, min=-reach, max=reach).astype(dtype)


def setup_inputs(seed: int = 0) -> dict:
    key_of = jax.random.split(jax.random.key(seed), 5)
    return {
        "velocity": draw_velocity(jax.random.fold_in(key_of[4], 71), 0),
        "geometry": scatter_about(key_of[1], (4, Q * Q, E_ALL), 0.5, 3.0, ((2, 8),), jnp.float32),
        "jacobian": jnp.clip(jnp.exp(math.log(2.0) - 1.3862944 * jax.random.uniform(key_of[2], (Q * Q, E_ALL), jnp.float32) ** shard_levels(key_of[2], (Q * Q, E_ALL), ((1, 8),), -0.2, 0.2)), 0.5, 2.0),
        "frame_flip": place_ends(jax.random.randint(key_of[3], (N_ELEM,), 0, 2), jax.random.fold_in(key_of[3], 1), 0, 1).astype(jnp.int32),
    }


spanwise_scale = 0.25
svv_cutoff = 4.0
svv_peak = 2.0
sensor_centre = -1.5
sensor_width = 0.6
energy_floor = 1e-6


def modal_basis(top_degree, points):
    legendre = [points * 0.0 + 1.0, points * 1.0]
    for order in range(1, top_degree):
        legendre.append(((2.0 * order + 1.0) * points * legendre[order] - order * legendre[order - 1]) / (order + 1.0))
    values = np.zeros((points.shape[0], top_degree + 1))
    slopes = np.zeros((points.shape[0], top_degree + 1))
    values[:, 0] = 0.5 * (1.0 - points)
    values[:, 1] = 0.5 * (1.0 + points)
    slopes[:, 0] = -0.5
    slopes[:, 1] = 0.5
    for column in range(2, top_degree + 1):
        values[:, column] = (legendre[column - 2] - points * legendre[column - 1]) / column
        slopes[:, column] = -legendre[column - 1]
    return values, slopes


def spectral_tables(top_degree, point_count, planes):
    fine_planes = 3 * planes // 2
    angles_q = np.pi * (np.arange(point_count) + 0.5) / point_count
    points = -np.cos(angles_q)
    series = np.arange(1, point_count // 2 + 1)
    weights = 2.0 / point_count * (1.0 - 2.0 * np.sum(np.cos(2.0 * series[None, :] * angles_q[:, None]) / (4.0 * series[None, :] ** 2 - 1.0), axis=1))
    values, slopes = modal_basis(top_degree, points)
    value_table = np.kron(values, values)
    xi_table = np.kron(slopes, values)
    eta_table = np.kron(values, slopes)
    point_weights = np.kron(weights, weights)
    degrees = np.maximum(np.arange(top_degree + 1), 1) * 1.0
    highest = np.maximum(degrees[:, None], degrees[None, :]).reshape(-1)
    tail_mask = (highest > svv_cutoff) * 1.0
    kernel = np.where(degrees > svv_cutoff, np.exp(-((top_degree - degrees) / np.maximum(degrees - svv_cutoff, 1.0)) ** 2), 0.0)
    per_dir = degrees * (degrees + 1.0) * kernel
    svv_weight = (per_dir[:, None] + per_dir[None, :]).reshape(-1) / (top_degree * (top_degree + 1.0))
    angles_z = 2.0 * np.pi * np.arange(fine_planes) / fine_planes
    coef_index = np.arange(planes)
    wavenumber = np.where(coef_index == 1, planes // 2, coef_index // 2)
    cosine_part = (coef_index % 2 == 0) | (coef_index == 1)
    inverse = np.where(cosine_part[None, :], np.cos(wavenumber[None, :] * angles_z[:, None]), np.sin(wavenumber[None, :] * angles_z[:, None]))
    forward = inverse.T * np.where(coef_index == 0, 1.0 / fine_planes, 2.0 / fine_planes)[:, None]
    tables = (value_table, xi_table, eta_table, point_weights, tail_mask, svv_weight, inverse, forward)
    return tuple(jnp.asarray(table.astype(np.float32)) for table in tables)


def z_slope(coeffs, wavenumbers):
    fields, planes, mode_count, elements = coeffs.shape
    paired = coeffs.reshape(fields, planes // 2, 2, mode_count, elements)
    factor = (spanwise_scale * wavenumbers)[None, :, None, None]
    slope = jnp.stack([factor * paired[:, :, 1], -factor * paired[:, :, 0]], axis=2)
    return slope.reshape(coeffs.shape)


def point_values(coeffs, zcoeffs, geometry, value_table, xi_table, eta_table):
    highest = lax.Precision.HIGHEST
    values = jnp.einsum('qm,fjme->fjqe', value_table, coeffs, precision=highest)
    along_xi = jnp.einsum('qm,fjme->fjqe', xi_table, coeffs, precision=highest)
    along_eta = jnp.einsum('qm,fjme->fjqe', eta_table, coeffs, precision=highest)
    along_z = jnp.einsum('qm,fjme->fjqe', value_table, zcoeffs, precision=highest)
    slope_x = geometry[0] * along_xi + geometry[1] * along_eta
    slope_y = geometry[2] * along_xi + geometry[3] * along_eta
    return jnp.concatenate([values, slope_x, slope_y, along_z], axis=0)


def advect(stacked, inverse, forward):
    highest = lax.Precision.HIGHEST
    physical = jnp.einsum('nj,cjqe->cnqe', inverse, stacked, precision=highest)
    speeds = physical[0:3]
    product = speeds[0] * physical[3:6] + speeds[1] * physical[6:9] + speeds[2] * physical[9:12]
    return jnp.einsum('jn,fnqe->fjqe', forward, product, precision=highest)


def project(nonlinear, jacobian, value_table, point_weights):
    weighted = nonlinear * (jacobian * point_weights[:, None])
    return jnp.einsum('qm,fjqe->fjme', value_table, weighted, precision=lax.Precision.HIGHEST)


def energies(coeffs, tail_mask):
    squares = coeffs * coeffs
    tail_energy = jnp.sum(squares * tail_mask[:, None], axis=(0, 1, 2))
    all_energy = jnp.sum(squares, axis=(0, 1, 2))
    return tail_energy, all_energy


def strength_ramp(tail_energy, all_energy):
    log_share = jnp.log((tail_energy + energy_floor) / (all_energy + energy_floor))
    return svv_peak * jax.nn.sigmoid((log_share - sensor_centre) / sensor_width)


def flip_edge(edge_modes):
    count_r = edge_modes.shape[2]
    parity = jnp.where(jnp.arange(2, count_r) % 2 == 0, 1.0, -1.0).astype(jnp.float32)
    parity = parity.reshape((-1,) + (1,) * (edge_modes.ndim - 3))
    swapped = jnp.concatenate([edge_modes[:, :, 1:2], edge_modes[:, :, 0:1], edge_modes[:, :, 2:] * parity], axis=2)
    return jnp.flip(swapped, axis=-1)


def assemble(weak_rhs, frame_flip):
    fields, planes = weak_rhs.shape[0], weak_rhs.shape[1]
    side = P_SIZE + 1
    modal_grid = weak_rhs.reshape(fields, planes, side, side, N_ELEM, EX, EY)
    left_modes = modal_grid[:, :, 0]
    right_modes = modal_grid[:, :, 1]
    flipped = (frame_flip == 1)[:, None]

    def canonical(edge_modes):
        return jnp.where(flipped, flip_edge(edge_modes), edge_modes)

    out_right = canonical(right_modes[:, :, :, :, -1])
    out_left = canonical(left_modes[:, :, :, :, 0])
    no_edge = jnp.zeros_like(out_right[:, :, :, :1])
    from_left = canonical(jnp.concatenate([no_edge, out_right[:, :, :, :-1]], axis=3))
    from_right = canonical(jnp.concatenate([out_left[:, :, :, 1:], no_edge], axis=3))
    left_next = jnp.concatenate([left_modes[:, :, :, :, 1:], from_right[:, :, :, :, None]], axis=4)
    right_prev = jnp.concatenate([from_left[:, :, :, :, None], right_modes[:, :, :, :, :-1]], axis=4)
    modal_grid = jnp.concatenate([(left_modes + right_prev)[:, :, None], (right_modes + left_next)[:, :, None], modal_grid[:, :, 2:]], axis=2)
    bottom = modal_grid[:, :, :, 0]
    top = modal_grid[:, :, :, 1]
    no_row = jnp.zeros_like(bottom[..., :1])
    new_bottom = bottom + jnp.concatenate([no_row, top[..., :-1]], axis=-1)
    new_top = top + jnp.concatenate([bottom[..., 1:], no_row], axis=-1)
    modal_grid = jnp.concatenate([new_bottom[:, :, :, None], new_top[:, :, :, None], modal_grid[:, :, :, 2:]], axis=3)
    return modal_grid.reshape(weak_rhs.shape)


def reference(velocity, geometry, jacobian, frame_flip):
    value_table, xi_table, eta_table, point_weights, tail_mask, svv_weight, inverse, forward = spectral_tables(P_SIZE, Q, NZ)
    block = EX * EY
    mode_count = velocity.shape[2]
    vel_blocks = velocity.reshape(3, NZ, mode_count, N_ELEM, block).transpose(3, 0, 1, 2, 4)
    geo_blocks = geometry.reshape(4, Q * Q, N_ELEM, block).transpose(2, 0, 1, 3)
    jac_blocks = jacobian.reshape(Q * Q, N_ELEM, block).transpose(1, 0, 2)
    wavenumbers = jnp.arange(NZ // 2).astype(jnp.float32)

    def one_block(inputs):
        coeffs, geom_here, jac_here = inputs
        zcoeffs = z_slope(coeffs, wavenumbers)
        stacked = point_values(coeffs, zcoeffs, geom_here, value_table, xi_table, eta_table)
        nonlinear = advect(stacked, inverse, forward)
        weak_rhs = project(nonlinear, jac_here, value_table, point_weights)
        tail_energy, all_energy = energies(coeffs, tail_mask)
        strength = strength_ramp(tail_energy, all_energy)
        damping = -strength[None, None, None, :] * svv_weight[None, None, :, None] * coeffs
        return weak_rhs, damping

    weak_blocks, damp_blocks = lax.map(one_block, (vel_blocks, geo_blocks, jac_blocks))
    weak_rhs = weak_blocks.transpose(1, 2, 3, 0, 4).reshape(velocity.shape)
    svv_force = damp_blocks.transpose(1, 2, 3, 0, 4).reshape(velocity.shape)
    advection = assemble(weak_rhs, frame_flip)
    return advection, svv_force
```

```python
import functools

import jax
import jax.numpy as jnp
import numpy as np
from jax import lax
from jax.experimental import pallas as pl
from jax.experimental.pallas import tpu as pltpu
from jax.sharding import PartitionSpec as P

P_SIZE = 8
Q = 10
NZ = 64
EY = 8


spanwise_scale = 0.25
svv_cutoff = 4.0
svv_peak = 2.0
sensor_centre = -1.5
sensor_width = 0.6
energy_floor = 1e-06


def from_behind(block, axis, distance):
    devices = range(lax.axis_size(axis))
    route = [(i - distance, i) for i in devices if i - distance in devices]
    return lax.ppermute(block, axis, route)


def modal_basis(top_degree, points):
    legendre = [points * 0.0 + 1.0, points * 1.0]
    for order in range(1, top_degree):
        legendre.append(
            ((2.0 * order + 1.0) * points * legendre[order] - order * legendre[order - 1])
            / (order + 1.0)
        )
    values = np.zeros((points.shape[0], top_degree + 1))
    slopes = np.zeros((points.shape[0], top_degree + 1))
    values[:, 0] = 0.5 * (1.0 - points)
    values[:, 1] = 0.5 * (1.0 + points)
    slopes[:, 0] = -0.5
    slopes[:, 1] = 0.5
    for column in range(2, top_degree + 1):
        values[:, column] = (legendre[column - 2] - points * legendre[column - 1]) / column
        slopes[:, column] = -legendre[column - 1]
    return (values, slopes)


def spectral_tables(top_degree, point_count, planes):
    fine_planes = 3 * planes // 2
    angles_q = np.pi * (np.arange(point_count) + 0.5) / point_count
    points = -np.cos(angles_q)
    series = np.arange(1, point_count // 2 + 1)
    weights = (
        2.0
        / point_count
        * (
            1.0
            - 2.0
            * np.sum(
                np.cos(2.0 * series[None, :] * angles_q[:, None])
                / (4.0 * series[None, :] ** 2 - 1.0),
                axis=1,
            )
        )
    )
    values, slopes = modal_basis(top_degree, points)
    value_table = np.kron(values, values)
    xi_table = np.kron(slopes, values)
    eta_table = np.kron(values, slopes)
    point_weights = np.kron(weights, weights)
    degrees = np.maximum(np.arange(top_degree + 1), 1) * 1.0
    highest = np.maximum(degrees[:, None], degrees[None, :]).reshape(-1)
    tail_mask = (highest > svv_cutoff) * 1.0
    kernel = np.where(
        degrees > svv_cutoff,
        np.exp(-(((top_degree - degrees) / np.maximum(degrees - svv_cutoff, 1.0)) ** 2)),
        0.0,
    )
    per_dir = degrees * (degrees + 1.0) * kernel
    svv_weight = (per_dir[:, None] + per_dir[None, :]).reshape(-1) / (
        top_degree * (top_degree + 1.0)
    )
    angles_z = 2.0 * np.pi * np.arange(fine_planes) / fine_planes
    coef_index = np.arange(planes)
    wavenumber = np.where(coef_index == 1, planes // 2, coef_index // 2)
    cosine_part = (coef_index % 2 == 0) | (coef_index == 1)
    inverse = np.where(
        cosine_part[None, :],
        np.cos(wavenumber[None, :] * angles_z[:, None]),
        np.sin(wavenumber[None, :] * angles_z[:, None]),
    )
    forward = inverse.T * np.where(coef_index == 0, 1.0 / fine_planes, 2.0 / fine_planes)[:, None]
    return (
        value_table,
        xi_table,
        eta_table,
        point_weights,
        tail_mask,
        svv_weight,
        inverse,
        forward,
    )


def z_slope(coeffs, wavenumbers):
    fields, planes, mode_count, elements = coeffs.shape
    paired = coeffs.reshape(fields, planes // 2, 2, mode_count, elements)
    factor = (spanwise_scale * wavenumbers)[None, :, None, None]
    slope = jnp.stack([factor * paired[:, :, 1], -factor * paired[:, :, 0]], axis=2)
    return slope.reshape(coeffs.shape)


def point_values(coeffs, zcoeffs, geometry, value_table, xi_table, eta_table):
    highest = lax.Precision.HIGHEST
    values = jnp.einsum("qm,fjme->fjqe", value_table, coeffs, precision=highest)
    along_xi = jnp.einsum("qm,fjme->fjqe", xi_table, coeffs, precision=highest)
    along_eta = jnp.einsum("qm,fjme->fjqe", eta_table, coeffs, precision=highest)
    along_z = jnp.einsum("qm,fjme->fjqe", value_table, zcoeffs, precision=highest)
    slope_x = geometry[0] * along_xi + geometry[1] * along_eta
    slope_y = geometry[2] * along_xi + geometry[3] * along_eta
    return jnp.concatenate([values, slope_x, slope_y, along_z], axis=0)


def advect(stacked, inverse, forward):
    highest = lax.Precision.HIGHEST
    physical = jnp.einsum("nj,cjqe->cnqe", inverse, stacked, precision=highest)
    speeds = physical[0:3]
    product = speeds[0] * physical[3:6] + speeds[1] * physical[6:9] + speeds[2] * physical[9:12]
    return jnp.einsum("jn,fnqe->fjqe", forward, product, precision=highest)


def project(nonlinear, jacobian, value_table, point_weights):
    weighted = nonlinear * (jacobian * point_weights[:, None])
    return jnp.einsum("qm,fjqe->fjme", value_table, weighted, precision=lax.Precision.HIGHEST)


def energies(coeffs, tail_mask):
    squares = coeffs * coeffs
    tail_energy = jnp.sum(squares * tail_mask[:, None], axis=(0, 1, 2))
    all_energy = jnp.sum(squares, axis=(0, 1, 2))
    return (tail_energy, all_energy)


def strength_ramp(tail_energy, all_energy):
    log_share = jnp.log((tail_energy + energy_floor) / (all_energy + energy_floor))
    return svv_peak * jax.nn.sigmoid((log_share - sensor_centre) / sensor_width)


def flip_edge(edge_modes):
    count_r = edge_modes.shape[2]
    parity = jnp.where(jnp.arange(2, count_r) % 2 == 0, 1.0, -1.0).astype(jnp.float32)
    parity = parity.reshape((-1,) + (1,) * (edge_modes.ndim - 3))
    swapped = jnp.concatenate(
        [edge_modes[:, :, 1:2], edge_modes[:, :, 0:1], edge_modes[:, :, 2:] * parity], axis=2
    )
    return jnp.flip(swapped, axis=-1)


def to_points(stacked):
    return lax.all_to_all(stacked, "plane", split_axis=3, concat_axis=1, tiled=True)


def to_planes(returned):
    return lax.all_to_all(returned, "plane", split_axis=1, concat_axis=3, tiled=True)


def assemble(weak_rhs, flip_flag):
    fields, planes, mode_count, elements = weak_rhs.shape
    side = P_SIZE + 1
    columns = elements // EY
    modal_grid = weak_rhs.reshape(fields, planes, side, side, columns, EY)
    left_modes = modal_grid[:, :, 0]
    right_modes = modal_grid[:, :, 1]
    flipped = flip_flag == 1

    def canonical(edge_modes):
        return jnp.where(flipped, flip_edge(edge_modes), edge_modes)

    out_right = canonical(right_modes[:, :, :, -1])
    out_left = canonical(left_modes[:, :, :, 0])
    from_left = canonical(from_behind(out_right, "elem", 1))
    from_right = canonical(from_behind(out_left, "elem", -1))
    left_next = jnp.concatenate([left_modes[:, :, :, 1:], from_right[:, :, :, None]], axis=3)
    right_prev = jnp.concatenate([from_left[:, :, :, None], right_modes[:, :, :, :-1]], axis=3)
    modal_grid = jnp.concatenate(
        [
            (left_modes + right_prev)[:, :, None],
            (right_modes + left_next)[:, :, None],
            modal_grid[:, :, 2:],
        ],
        axis=2,
    )
    bottom = modal_grid[:, :, :, 0]
    top = modal_grid[:, :, :, 1]
    no_row = jnp.zeros_like(bottom[..., :1])
    new_bottom = bottom + jnp.concatenate([no_row, top[..., :-1]], axis=-1)
    new_top = top + jnp.concatenate([bottom[..., 1:], no_row], axis=-1)
    modal_grid = jnp.concatenate(
        [new_bottom[:, :, :, None], new_top[:, :, :, None], modal_grid[:, :, :, 2:]], axis=3
    )
    return modal_grid.reshape(weak_rhs.shape)


MODES = (P_SIZE + 1) * (P_SIZE + 1)
POINTS = Q * Q
FINE = 3 * NZ // 2
WIDE = 256
LANES = 128
CHUNKS = 2
MESH = pl.DeviceIdType.MESH


def halves(table):
    high = table.astype(np.float32).astype(jnp.bfloat16)
    low = (table - high.astype(np.float64)).astype(jnp.bfloat16)
    return high, low


def kernel_tables():
    value, xi, eta, weights, tail, svv, inverse, forward = spectral_tables(P_SIZE, Q, NZ)
    to_point = np.zeros((WIDE, 9 * LANES))
    to_mode = np.zeros((3 * LANES, WIDE))
    for field in range(3):
        rows = slice(field * MODES, (field + 1) * MODES)
        for kind, table in enumerate((value, xi, eta)):
            start = (kind * 3 + field) * LANES
            to_point[rows, start : start + POINTS] = table.T
        to_mode[field * LANES : field * LANES + POINTS, rows] = value
    slope = np.zeros((FINE, NZ))
    for m in range(1, NZ // 2):
        slope[:, 2 * m + 1] = spanwise_scale * m * inverse[:, 2 * m]
        slope[:, 2 * m] = -spanwise_scale * m * inverse[:, 2 * m + 1]

    def triple(table):
        high, low = halves(table)
        return np.concatenate([high, low, high], axis=1)

    lanes = np.zeros((8, WIDE), np.float32)
    lanes[0, : 3 * MODES] = np.tile(tail, 3)
    lanes[1, :MODES] = svv
    lanes[2, :POINTS] = weights
    edges = np.zeros((2, 2, 4, WIDE, LANES), np.float32)
    side = P_SIZE + 1
    for end in range(2):
        for slot in range(4):
            for field in range(3):
                for r in range(side):
                    source = field * MODES + end * side
                    edges[end, 0, slot, source + r, slot * 32 + field * side + r] = 1.0
                    swapped = 1 - r if r < 2 else r
                    sign = 1.0 if r < 2 or r % 2 == 0 else -1.0
                    edges[end, 1, slot, source + swapped, (3 - slot) * 32 + field * side + r] = sign
    edges = edges.reshape(4, 4 * WIDE, LANES).astype(jnp.bfloat16)
    return (
        *halves(to_point),
        *halves(to_mode),
        triple(inverse),
        triple(slope),
        triple(forward),
        lanes,
        edges,
    )


def split(x):
    high = x.astype(jnp.bfloat16)
    return high, (x - high.astype(jnp.float32)).astype(jnp.bfloat16)


def dot(a, b):
    return lax.dot_general(a, b, (((1,), (0,)), ((), ())), preferred_element_type=jnp.float32)


def dot_t(a, b):
    return lax.dot_general(a, b, (((1,), (1,)), ((), ())), preferred_element_type=jnp.float32)


def dot3(x, high, low):
    x_high, x_low = split(x)
    return dot(x_high, high) + dot(x_high, low) + dot(x_low, high)


def stacked_halves(x):
    high, low = split(x)
    return jnp.concatenate([high, high, low], axis=0)


def advance(n_plane, n_elem, flip_ref, vel_ref, geo_ref, jac_ref, ph_ref, pl_ref, mh_ref, ml_ref,
            inv_ref, slo_ref, fwd_ref, lane_ref, edge_ref, adv_ref, svv_ref,
            vel_s, pack_s, got_s, weight_s, energy_s, strength_s, point_s, hat_s, back_s, weak_s,
            edge_out, edge_in, out_s,
            send_a, recv_a, send_s, recv_s, send_b, recv_b, send_e, recv_e):
    block = lax.axis_index("elem")
    me = lax.axis_index("plane")
    planes = NZ // n_plane
    rows = EY
    columns = n_plane
    elements = rows * columns
    part = rows // CHUNKS
    offsets = [2, 1, 3]
    has_prev = block > 0
    has_next = block < n_elem - 1

    def peer(offset):
        return lax.rem(me + offset, n_plane)

    barrier = pltpu.get_barrier_semaphore()
    for offset in offsets:
        pl.semaphore_signal(barrier, inc=1, device_id=(block, peer(offset)), device_id_type=MESH)

    @pl.when(has_prev)
    def _():
        pl.semaphore_signal(barrier, inc=1, device_id=(block - 1, me), device_id_type=MESH)

    @pl.when(has_next)
    def _():
        pl.semaphore_signal(barrier, inc=1, device_id=(block + 1, me), device_id_type=MESH)

    for field in range(3):
        vel_s[field * planes * elements : (field + 1) * planes * elements, 0:MODES] = vel_ref[field]

    lane = lax.broadcasted_iota(jnp.int32, (planes, LANES), 1)
    first_cut = LANES - MODES

    def pack(target, element):
        base = target * rows + element
        u, v, w = [
            vel_s[pl.ds(field * planes * elements + base, planes, stride=elements), :]
            for field in range(3)
        ]
        v_turned = pltpu.roll(v, MODES, 1)
        w_turned = pltpu.roll(w, 2 * MODES - LANES, 1)
        left = jnp.where(lane < MODES, u, v_turned)
        right = jnp.where(
            lane < 2 * MODES - LANES, v_turned, jnp.where(lane < 3 * MODES - LANES, w_turned, 0.0)
        )
        return jnp.concatenate([left, right], axis=1)

    def forward_copy(i, chunk):
        span = pl.ds(chunk * part, part)
        return pltpu.make_async_remote_copy(
            src_ref=pack_s.at[i, span],
            dst_ref=got_s.at[me, span],
            send_sem=send_a.at[i, chunk],
            recv_sem=recv_a.at[i, chunk],
            device_id=(block, peer(offsets[i])),
            device_id_type=MESH,
        )

    def back_copy(i, chunk):
        span = pl.ds(chunk * part, part)
        return pltpu.make_async_remote_copy(
            src_ref=back_s.at[peer(offsets[i]), span],
            dst_ref=weak_s.at[me, span],
            send_sem=send_b.at[i, chunk],
            recv_sem=recv_b.at[i, chunk],
            device_id=(block, peer(offsets[i])),
            device_id_type=MESH,
        )

    def strength_copy(i):
        return pltpu.make_async_remote_copy(
            src_ref=strength_s.at[n_plane],
            dst_ref=strength_s.at[me],
            send_sem=send_s.at[i],
            recv_sem=recv_s.at[i],
            device_id=(block, peer(offsets[i])),
            device_id_type=MESH,
        )

    def edge_copy(i, target):
        return pltpu.make_async_remote_copy(
            src_ref=edge_out.at[i],
            dst_ref=edge_in.at[i],
            send_sem=send_e.at[i],
            recv_sem=recv_e.at[i],
            device_id=(target, me),
            device_id_type=MESH,
        )

    for chunk in range(CHUNKS):
        for i, offset in enumerate(offsets):
            target = peer(offset)
            for element in range(chunk * part, (chunk + 1) * part):
                pack_s[i, element] = pack(target, element)
            if chunk == 0 and i == 0:
                pl.semaphore_wait(
                    barrier, len(offsets) + has_prev.astype(jnp.int32) + has_next.astype(jnp.int32)
                )
            forward_copy(i, chunk).start()
    for element in range(rows):
        got_s[me, element] = pack(me, element)

    start = pl.multiple_of(me * rows, 8)
    area = jac_ref[pl.ds(start, rows), :] * lane_ref[2:3, 0:POINTS]
    weight_s[...] = jnp.zeros_like(weight_s)
    for i in range(4):
        weight_s[i, :, 0:POINTS] = geo_ref[i, pl.ds(start, rows), :] * area
    weight_s[4, :, 0:POINTS] = area

    for chunk in range(CHUNKS):
        for i in range(len(offsets)):
            forward_copy(i, chunk).wait_recv()
        span = slice(chunk * part, (chunk + 1) * part)
        x = jnp.concatenate(
            [got_s[source, element] for element in range(chunk * part, (chunk + 1) * part)
             for source in range(n_plane)], axis=0)
        energy_s[span, :] = jnp.sum((x * x).reshape(part, NZ, WIDE), axis=1)
        point_s[...] = dot3(x, ph_ref[...], pl_ref[...])
        if chunk == CHUNKS - 1:
            squares = energy_s[...]
            tail_energy = jnp.sum(squares * lane_ref[0:1, :], axis=1, keepdims=True)
            all_energy = jnp.sum(squares, axis=1, keepdims=True)
            log_share = jnp.log((tail_energy + energy_floor) / (all_energy + energy_floor))
            ramp = (log_share - sensor_centre) / sensor_width
            strength = svv_peak / (1.0 + jnp.exp(-ramp))
            strength_s[n_plane] = jnp.broadcast_to(strength, (rows, LANES))
            strength_s[me] = jnp.broadcast_to(strength, (rows, LANES))
            for i in range(len(offsets)):
                strength_copy(i).start()

        for local in range(part):
            element = chunk * part + local
            here = slice(local * NZ, (local + 1) * NZ)
            u = point_s[here, 0:LANES]
            v = point_s[here, LANES : 2 * LANES]
            w = point_s[here, 2 * LANES : 3 * LANES]
            g = [weight_s[i, element : element + 1, :] for i in range(5)]
            carriers = jnp.concatenate([g[0] * u + g[2] * v, g[1] * u + g[3] * v, g[4] * w], axis=1)
            speeds = dot(inv_ref[...], stacked_halves(carriers))
            slopes = dot(inv_ref[...], stacked_halves(point_s[here, 3 * LANES :]))
            along_z = dot(slo_ref[...], stacked_halves(point_s[here, 0 : 3 * LANES]))
            product = jnp.concatenate(
                [
                    speeds[:, 0:LANES] * slopes[:, f * LANES : (f + 1) * LANES]
                    + speeds[:, LANES : 2 * LANES] * slopes[:, (3 + f) * LANES : (4 + f) * LANES]
                    + speeds[:, 2 * LANES :] * along_z[:, f * LANES : (f + 1) * LANES]
                    for f in range(3)
                ],
                axis=1,
            )
            hat_s[here, :] = dot(fwd_ref[...], stacked_halves(product))
        weak = dot3(hat_s[...], mh_ref[...], ml_ref[...])
        for local in range(part):
            for k in range(n_plane):
                first = local * NZ + k * planes
                back_s[k, chunk * part + local] = weak[first : first + planes]
        for i in range(len(offsets)):
            back_copy(i, chunk).start()
        for local in range(part):
            weak_s[me, chunk * part + local] = back_s[me, chunk * part + local]

    for i in range(len(offsets)):
        strength_copy(i).wait_recv()
    for column in range(columns):
        factor = -strength_s[column] * lane_ref[1:2, 0:LANES]
        for field in range(3):
            for j in range(planes):
                at = slice(j * elements + column * rows, j * elements + (column + 1) * rows)
                svv_ref[field, at, :] = vel_ref[field, at, :] * factor[:, 0:MODES]

    for chunk in range(CHUNKS):
        for i in range(len(offsets)):
            back_copy(i, chunk).wait_recv()

    flipped = flip_ref[0] == 1
    turn = jnp.where(flipped, 1, 0)
    for i, column in ((0, 0), (1, columns - 1)):
        table = edge_ref[2 * i + turn]
        tiles = []
        for half in range(2):
            picked = jnp.concatenate([weak_s[column, 4 * half + s] for s in range(4)], axis=1)
            high, low = split(picked)
            tiles.append(dot(high, table) + dot(low, table))
        edge_out[i, 0] = jnp.where(flipped, tiles[1], tiles[0])
        edge_out[i, 1] = jnp.where(flipped, tiles[0], tiles[1])

    @pl.when(has_prev)
    def _():
        edge_copy(0, block - 1).start()

    @pl.when(has_next)
    def _():
        edge_copy(1, block + 1).start()

    wide = lax.broadcasted_iota(jnp.int32, (planes, WIDE), 1)
    side = P_SIZE + 1
    inside = wide < 3 * MODES
    is_left = inside & (lax.rem(wide, MODES) < side)
    is_right = inside & (lax.rem(wide, MODES) >= side) & (lax.rem(wide, MODES) < 2 * side)
    is_bottom = inside & (lax.rem(wide, side) == 0)
    is_top = inside & (lax.rem(wide, side) == 1)

    for row in range(rows):
        strip = [weak_s[column, row] for column in range(columns)]
        for column in range(columns):
            total = strip[column]
            if column > 0:
                total = total + jnp.where(is_left, pltpu.roll(strip[column - 1], WIDE - side, 1), 0.0)
            if column < columns - 1:
                total = total + jnp.where(is_right, pltpu.roll(strip[column + 1], side, 1), 0.0)
            got_s[column, row] = total

    @pl.when(has_next)
    def _():
        edge_copy(0, block + 1).wait_recv()

    @pl.when(block == n_elem - 1)
    def _():
        edge_in[0] = jnp.zeros((2, planes, LANES), jnp.float32)

    @pl.when(has_prev)
    def _():
        edge_copy(1, block - 1).wait_recv()

    @pl.when(block == 0)
    def _():
        edge_in[1] = jnp.zeros((2, planes, LANES), jnp.float32)

    for i, column in ((1, 0), (0, columns - 1)):
        table = edge_ref[2 * (1 - i) + turn]
        for half in range(2):
            tile = jnp.where(flipped, edge_in[i, 1 - half], edge_in[i, half])
            high, low = split(tile)
            spread = dot_t(high, table) + dot_t(low, table)
            for s in range(4):
                got_s[column, 4 * half + s] += spread[:, s * WIDE : (s + 1) * WIDE]

    for column in range(columns):
        strip = [got_s[column, row] for row in range(rows)]
        for row in range(rows):
            total = strip[row]
            if row > 0:
                total = total + jnp.where(is_bottom, pltpu.roll(strip[row - 1], WIDE - 1, 1), 0.0)
            if row < rows - 1:
                total = total + jnp.where(is_top, pltpu.roll(strip[row + 1], 1, 1), 0.0)
            fields = (
                total[:, 0:LANES],
                pltpu.roll(total, WIDE - MODES, 1)[:, 0:LANES],
                pltpu.roll(total, WIDE - 2 * MODES, 1)[:, 0:LANES],
            )
            for field in range(3):
                base = field * planes * elements + column * rows + row
                out_s[pl.ds(base, planes, stride=elements), :] = fields[field]
    for field in range(3):
        adv_ref[field] = out_s[field * planes * elements : (field + 1) * planes * elements, 0:MODES]

    for i in range(len(offsets)):
        strength_copy(i).wait_send()
        for chunk in range(CHUNKS):
            forward_copy(i, chunk).wait_send()
            back_copy(i, chunk).wait_send()

    @pl.when(has_prev)
    def _():
        edge_copy(0, block - 1).wait_send()

    @pl.when(has_next)
    def _():
        edge_copy(1, block + 1).wait_send()


def kernel_body(n_plane, n_elem, velocity, geometry, jacobian, frame_flip):
    planes, elements = velocity.shape[1], velocity.shape[3]
    tables = [jnp.asarray(table) for table in kernel_tables()]
    vel = velocity.transpose(0, 1, 3, 2).reshape(3, planes * elements, MODES)
    geo = geometry.transpose(0, 2, 1)
    jac = jacobian.transpose(1, 0)
    whole = pl.BlockSpec(memory_space=pltpu.VMEM)
    part = EY // CHUNKS
    flat = jax.ShapeDtypeStruct((3, planes * elements, MODES), jnp.float32)
    f32 = jnp.float32
    dma = pltpu.SemaphoreType.DMA
    others = n_plane - 1
    advection, svv = pl.pallas_call(
        functools.partial(advance, n_plane, n_elem),
        out_shape=(flat, flat),
        in_specs=[pl.BlockSpec(memory_space=pltpu.SMEM)] + [whole] * (3 + len(tables)),
        out_specs=(whole, whole),
        scratch_shapes=[
            pltpu.VMEM((3 * planes * elements, LANES), f32),
            pltpu.VMEM((others, EY, planes, WIDE), f32),
            pltpu.VMEM((n_plane, EY, planes, WIDE), f32),
            pltpu.VMEM((5, EY, LANES), f32),
            pltpu.VMEM((EY, WIDE), f32),
            pltpu.VMEM((n_plane + 1, EY, LANES), f32),
            pltpu.VMEM((part * NZ, 9 * LANES), f32),
            pltpu.VMEM((part * NZ, 3 * LANES), f32),
            pltpu.VMEM((n_plane, EY, planes, WIDE), f32),
            pltpu.VMEM((n_plane, EY, planes, WIDE), f32),
            pltpu.VMEM((2, 2, planes, LANES), f32),
            pltpu.VMEM((2, 2, planes, LANES), f32),
            pltpu.VMEM((3 * planes * elements, LANES), f32),
            dma((others, CHUNKS)),
            dma((others, CHUNKS)),
            dma((others,)),
            dma((others,)),
            dma((others, CHUNKS)),
            dma((others, CHUNKS)),
            dma((2,)),
            dma((2,)),
        ],
        compiler_params=pltpu.CompilerParams(
            collective_id=0, has_side_effects=True, vmem_limit_bytes=40 * 1024 * 1024
        ),
    )(frame_flip, vel, geo, jac, *tables)

    def restore(x):
        return x.reshape(3, planes, elements, MODES).transpose(0, 1, 3, 2)

    return restore(advection), restore(svv)


def body(velocity, geometry, jacobian, frame_flip):
    value_table, xi_table, eta_table, point_weights, tail_mask, svv_weight, inverse, forward = (
        jnp.asarray(table.astype(np.float32)) for table in spectral_tables(P_SIZE, Q, NZ)
    )
    planes_here = velocity.shape[1]
    position = lax.axis_index("plane")
    wavenumbers = (position * (planes_here // 2) + jnp.arange(planes_here // 2)).astype(jnp.float32)
    zcoeffs = z_slope(velocity, wavenumbers)
    stacked = point_values(velocity, zcoeffs, geometry, value_table, xi_table, eta_table)
    gathered = to_points(stacked)
    nonlinear = advect(gathered, inverse, forward)
    returned = to_planes(nonlinear)
    weak_rhs = project(returned, jacobian, value_table, point_weights)
    tail_part, all_part = energies(velocity, tail_mask)
    tail_energy, all_energy = lax.psum((tail_part, all_part), "plane")
    strength = strength_ramp(tail_energy, all_energy)
    svv_force = -strength[None, None, None, :] * svv_weight[None, None, :, None] * velocity
    advection = assemble(weak_rhs, frame_flip[0])
    return (advection, svv_force)


def solution(mesh):
    n_plane, n_elem = mesh.shape["plane"], mesh.shape["elem"]
    fits = n_plane == 4 and (NZ // n_plane) % 16 == 0
    return jax.shard_map(
        functools.partial(kernel_body, n_plane, n_elem) if fits else body,
        mesh=mesh,
        in_specs=(
            P(None, "plane", None, "elem"),
            P(None, None, "elem"),
            P(None, "elem"),
            P("elem"),
        ),
        out_specs=(P(None, "plane", None, "elem"), P(None, "plane", None, "elem")),
        check_vma=False,
    )
```

```python
import functools

import jax
import jax.numpy as jnp
import numpy as np
from jax import lax
from jax.experimental import pallas as pl
from jax.experimental.pallas import tpu as pltpu
from jax.sharding import PartitionSpec as P

P_SIZE = 8
Q = 10
NZ = 64
EY = 8


spanwise_scale = 0.25
svv_cutoff = 4.0
svv_peak = 2.0
sensor_centre = -1.5
sensor_width = 0.6
energy_floor = 1e-06


def from_behind(block, axis, distance):
    devices = range(lax.axis_size(axis))
    route = [(i - distance, i) for i in devices if i - distance in devices]
    return lax.ppermute(block, axis, route)


def modal_basis(top_degree, points):
    legendre = [points * 0.0 + 1.0, points * 1.0]
    for order in range(1, top_degree):
        legendre.append(
            ((2.0 * order + 1.0) * points * legendre[order] - order * legendre[order - 1])
            / (order + 1.0)
        )
    values = np.zeros((points.shape[0], top_degree + 1))
    slopes = np.zeros((points.shape[0], top_degree + 1))
    values[:, 0] = 0.5 * (1.0 - points)
    values[:, 1] = 0.5 * (1.0 + points)
    slopes[:, 0] = -0.5
    slopes[:, 1] = 0.5
    for column in range(2, top_degree + 1):
        values[:, column] = (legendre[column - 2] - points * legendre[column - 1]) / column
        slopes[:, column] = -legendre[column - 1]
    return (values, slopes)


def spectral_tables(top_degree, point_count, planes):
    fine_planes = 3 * planes // 2
    angles_q = np.pi * (np.arange(point_count) + 0.5) / point_count
    points = -np.cos(angles_q)
    series = np.arange(1, point_count // 2 + 1)
    weights = (
        2.0
        / point_count
        * (
            1.0
            - 2.0
            * np.sum(
                np.cos(2.0 * series[None, :] * angles_q[:, None])
                / (4.0 * series[None, :] ** 2 - 1.0),
                axis=1,
            )
        )
    )
    values, slopes = modal_basis(top_degree, points)
    value_table = np.kron(values, values)
    xi_table = np.kron(slopes, values)
    eta_table = np.kron(values, slopes)
    point_weights = np.kron(weights, weights)
    degrees = np.maximum(np.arange(top_degree + 1), 1) * 1.0
    highest = np.maximum(degrees[:, None], degrees[None, :]).reshape(-1)
    tail_mask = (highest > svv_cutoff) * 1.0
    kernel = np.where(
        degrees > svv_cutoff,
        np.exp(-(((top_degree - degrees) / np.maximum(degrees - svv_cutoff, 1.0)) ** 2)),
        0.0,
    )
    per_dir = degrees * (degrees + 1.0) * kernel
    svv_weight = (per_dir[:, None] + per_dir[None, :]).reshape(-1) / (
        top_degree * (top_degree + 1.0)
    )
    angles_z = 2.0 * np.pi * np.arange(fine_planes) / fine_planes
    coef_index = np.arange(planes)
    wavenumber = np.where(coef_index == 1, planes // 2, coef_index // 2)
    cosine_part = (coef_index % 2 == 0) | (coef_index == 1)
    inverse = np.where(
        cosine_part[None, :],
        np.cos(wavenumber[None, :] * angles_z[:, None]),
        np.sin(wavenumber[None, :] * angles_z[:, None]),
    )
    forward = inverse.T * np.where(coef_index == 0, 1.0 / fine_planes, 2.0 / fine_planes)[:, None]
    return (
        value_table,
        xi_table,
        eta_table,
        point_weights,
        tail_mask,
        svv_weight,
        inverse,
        forward,
    )


def z_slope(coeffs, wavenumbers):
    fields, planes, mode_count, elements = coeffs.shape
    paired = coeffs.reshape(fields, planes // 2, 2, mode_count, elements)
    factor = (spanwise_scale * wavenumbers)[None, :, None, None]
    slope = jnp.stack([factor * paired[:, :, 1], -factor * paired[:, :, 0]], axis=2)
    return slope.reshape(coeffs.shape)


def point_values(coeffs, zcoeffs, geometry, value_table, xi_table, eta_table):
    highest = lax.Precision.HIGHEST
    values = jnp.einsum("qm,fjme->fjqe", value_table, coeffs, precision=highest)
    along_xi = jnp.einsum("qm,fjme->fjqe", xi_table, coeffs, precision=highest)
    along_eta = jnp.einsum("qm,fjme->fjqe", eta_table, coeffs, precision=highest)
    along_z = jnp.einsum("qm,fjme->fjqe", value_table, zcoeffs, precision=highest)
    slope_x = geometry[0] * along_xi + geometry[1] * along_eta
    slope_y = geometry[2] * along_xi + geometry[3] * along_eta
    return jnp.concatenate([values, slope_x, slope_y, along_z], axis=0)


def advect(stacked, inverse, forward):
    highest = lax.Precision.HIGHEST
    physical = jnp.einsum("nj,cjqe->cnqe", inverse, stacked, precision=highest)
    speeds = physical[0:3]
    product = speeds[0] * physical[3:6] + speeds[1] * physical[6:9] + speeds[2] * physical[9:12]
    return jnp.einsum("jn,fnqe->fjqe", forward, product, precision=highest)


def project(nonlinear, jacobian, value_table, point_weights):
    weighted = nonlinear * (jacobian * point_weights[:, None])
    return jnp.einsum("qm,fjqe->fjme", value_table, weighted, precision=lax.Precision.HIGHEST)


def energies(coeffs, tail_mask):
    squares = coeffs * coeffs
    tail_energy = jnp.sum(squares * tail_mask[:, None], axis=(0, 1, 2))
    all_energy = jnp.sum(squares, axis=(0, 1, 2))
    return (tail_energy, all_energy)


def strength_ramp(tail_energy, all_energy):
    log_share = jnp.log((tail_energy + energy_floor) / (all_energy + energy_floor))
    return svv_peak * jax.nn.sigmoid((log_share - sensor_centre) / sensor_width)


def flip_edge(edge_modes):
    count_r = edge_modes.shape[2]
    parity = jnp.where(jnp.arange(2, count_r) % 2 == 0, 1.0, -1.0).astype(jnp.float32)
    parity = parity.reshape((-1,) + (1,) * (edge_modes.ndim - 3))
    swapped = jnp.concatenate(
        [edge_modes[:, :, 1:2], edge_modes[:, :, 0:1], edge_modes[:, :, 2:] * parity], axis=2
    )
    return jnp.flip(swapped, axis=-1)


def to_points(stacked):
    return lax.all_to_all(stacked, "plane", split_axis=3, concat_axis=1, tiled=True)


def to_planes(returned):
    return lax.all_to_all(returned, "plane", split_axis=1, concat_axis=3, tiled=True)


def assemble(weak_rhs, flip_flag):
    fields, planes, mode_count, elements = weak_rhs.shape
    side = P_SIZE + 1
    columns = elements // EY
    modal_grid = weak_rhs.reshape(fields, planes, side, side, columns, EY)
    left_modes = modal_grid[:, :, 0]
    right_modes = modal_grid[:, :, 1]
    flipped = flip_flag == 1

    def canonical(edge_modes):
        return jnp.where(flipped, flip_edge(edge_modes), edge_modes)

    out_right = canonical(right_modes[:, :, :, -1])
    out_left = canonical(left_modes[:, :, :, 0])
    from_left = canonical(from_behind(out_right, "elem", 1))
    from_right = canonical(from_behind(out_left, "elem", -1))
    left_next = jnp.concatenate([left_modes[:, :, :, 1:], from_right[:, :, :, None]], axis=3)
    right_prev = jnp.concatenate([from_left[:, :, :, None], right_modes[:, :, :, :-1]], axis=3)
    modal_grid = jnp.concatenate(
        [
            (left_modes + right_prev)[:, :, None],
            (right_modes + left_next)[:, :, None],
            modal_grid[:, :, 2:],
        ],
        axis=2,
    )
    bottom = modal_grid[:, :, :, 0]
    top = modal_grid[:, :, :, 1]
    no_row = jnp.zeros_like(bottom[..., :1])
    new_bottom = bottom + jnp.concatenate([no_row, top[..., :-1]], axis=-1)
    new_top = top + jnp.concatenate([bottom[..., 1:], no_row], axis=-1)
    modal_grid = jnp.concatenate(
        [new_bottom[:, :, :, None], new_top[:, :, :, None], modal_grid[:, :, :, 2:]], axis=3
    )
    return modal_grid.reshape(weak_rhs.shape)


MODES = (P_SIZE + 1) * (P_SIZE + 1)
POINTS = Q * Q
FINE = 3 * NZ // 2
WIDE = 256
LANES = 128
CHUNKS = 2
TABLES = 9
MESH = pl.DeviceIdType.MESH


def halves(table):
    high = table.astype(np.float32).astype(jnp.bfloat16)
    low = (table - high.astype(np.float64)).astype(jnp.bfloat16)
    return high, low


def kernel_tables():
    value, xi, eta, weights, tail, svv, inverse, forward = spectral_tables(P_SIZE, Q, NZ)
    to_point = np.zeros((WIDE, 9 * LANES))
    to_mode = np.zeros((3 * LANES, WIDE))
    for field in range(3):
        rows = slice(field * MODES, (field + 1) * MODES)
        for kind, table in enumerate((value, xi, eta)):
            start = (kind * 3 + field) * LANES
            to_point[rows, start : start + POINTS] = table.T
        to_mode[field * LANES : field * LANES + POINTS, rows] = value
    slope = np.zeros((FINE, NZ))
    for m in range(1, NZ // 2):
        slope[:, 2 * m + 1] = spanwise_scale * m * inverse[:, 2 * m]
        slope[:, 2 * m] = -spanwise_scale * m * inverse[:, 2 * m + 1]

    def triple(table):
        high, low = halves(table)
        return np.concatenate([high, low, high], axis=1)

    lanes = np.zeros((8, WIDE), np.float32)
    lanes[0, : 3 * MODES] = np.tile(tail, 3)
    lanes[1, :MODES] = svv
    lanes[2, :POINTS] = weights
    edges = np.zeros((2, 2, 4, WIDE, LANES), np.float32)
    side = P_SIZE + 1
    for end in range(2):
        for slot in range(4):
            for field in range(3):
                for r in range(side):
                    source = field * MODES + end * side
                    edges[end, 0, slot, source + r, slot * 32 + field * side + r] = 1.0
                    swapped = 1 - r if r < 2 else r
                    sign = 1.0 if r < 2 or r % 2 == 0 else -1.0
                    edges[end, 1, slot, source + swapped, (3 - slot) * 32 + field * side + r] = sign
    edges = edges.reshape(4, 4 * WIDE, LANES).astype(jnp.bfloat16)
    return (
        lanes,
        *halves(to_point),
        triple(inverse),
        triple(slope),
        triple(forward),
        *halves(to_mode),
        edges,
    )


def split(x):
    high = x.astype(jnp.bfloat16)
    return high, (x - high.astype(jnp.float32)).astype(jnp.bfloat16)


def dot(a, b):
    return lax.dot_general(a, b, (((1,), (0,)), ((), ())), preferred_element_type=jnp.float32)


def dot_t(a, b):
    return lax.dot_general(a, b, (((1,), (1,)), ((), ())), preferred_element_type=jnp.float32)


def dot3(x, high, low):
    x_high, x_low = split(x)
    return dot(x_high, high) + dot(x_high, low) + dot(x_low, high)


def stacked_halves(x):
    high, low = split(x)
    return jnp.concatenate([high, high, low], axis=0)


def advance(n_plane, n_elem, flip_ref, *refs):
    n_in = 3 + TABLES
    sources, (adv_ref, svv_ref), held = refs[:n_in], refs[n_in : n_in + 2], refs[n_in + 2 : 2 * n_in + 2]
    fetches = [
        pltpu.make_async_copy(source, target, refs[-1].at[i])
        for i, (source, target) in enumerate(zip(sources, held))
    ]
    for fetch in fetches:
        fetch.start()
    advance_block(n_plane, n_elem, fetches, flip_ref, *held, adv_ref, svv_ref, *refs[2 * n_in + 2 : -1])


def advance_block(n_plane, n_elem, fetches, flip_ref, vel_ref, geo_ref, jac_ref, lane_ref, ph_ref,
            pl_ref, inv_ref, slo_ref, fwd_ref, mh_ref, ml_ref, edge_ref, adv_ref, svv_ref,
            vel_s, pack_s, got_s, weight_s, energy_s, strength_s, point_s, hat_s, back_s, weak_s,
            edge_out, edge_in, out_s,
            send_a, recv_a, send_s, recv_s, send_b, recv_b, send_e, recv_e):
    block = lax.axis_index("elem")
    me = lax.axis_index("plane")
    planes = NZ // n_plane
    rows = EY
    columns = n_plane
    elements = rows * columns
    part = rows // CHUNKS
    offsets = [2, 1, 3]
    has_prev = block > 0
    has_next = block < n_elem - 1

    def peer(offset):
        return lax.rem(me + offset, n_plane)

    barrier = pltpu.get_barrier_semaphore()
    for offset in offsets:
        pl.semaphore_signal(barrier, inc=1, device_id=(block, peer(offset)), device_id_type=MESH)

    @pl.when(has_prev)
    def _():
        pl.semaphore_signal(barrier, inc=1, device_id=(block - 1, me), device_id_type=MESH)

    @pl.when(has_next)
    def _():
        pl.semaphore_signal(barrier, inc=1, device_id=(block + 1, me), device_id_type=MESH)

    fetches[0].wait()
    for field in range(3):
        vel_s[field * planes * elements : (field + 1) * planes * elements, 0:MODES] = vel_ref[field]

    lane = lax.broadcasted_iota(jnp.int32, (planes, LANES), 1)
    first_cut = LANES - MODES

    def pack(target, element):
        base = target * rows + element
        u, v, w = [
            vel_s[pl.ds(field * planes * elements + base, planes, stride=elements), :]
            for field in range(3)
        ]
        v_turned = pltpu.roll(v, MODES, 1)
        w_turned = pltpu.roll(w, 2 * MODES - LANES, 1)
        left = jnp.where(lane < MODES, u, v_turned)
        right = jnp.where(
            lane < 2 * MODES - LANES, v_turned, jnp.where(lane < 3 * MODES - LANES, w_turned, 0.0)
        )
        return jnp.concatenate([left, right], axis=1)

    def forward_copy(i, chunk):
        span = pl.ds(chunk * part, part)
        return pltpu.make_async_remote_copy(
            src_ref=pack_s.at[i, span],
            dst_ref=got_s.at[me, span],
            send_sem=send_a.at[i, chunk],
            recv_sem=recv_a.at[i, chunk],
            device_id=(block, peer(offsets[i])),
            device_id_type=MESH,
        )

    def back_copy(i, chunk):
        span = pl.ds(chunk * part, part)
        return pltpu.make_async_remote_copy(
            src_ref=back_s.at[peer(offsets[i]), span],
            dst_ref=weak_s.at[me, span],
            send_sem=send_b.at[i, chunk],
            recv_sem=recv_b.at[i, chunk],
            device_id=(block, peer(offsets[i])),
            device_id_type=MESH,
        )

    def strength_copy(i):
        return pltpu.make_async_remote_copy(
            src_ref=strength_s.at[n_plane],
            dst_ref=strength_s.at[me],
            send_sem=send_s.at[i],
            recv_sem=recv_s.at[i],
            device_id=(block, peer(offsets[i])),
            device_id_type=MESH,
        )

    def edge_copy(i, target):
        return pltpu.make_async_remote_copy(
            src_ref=edge_out.at[i],
            dst_ref=edge_in.at[i],
            send_sem=send_e.at[i],
            recv_sem=recv_e.at[i],
            device_id=(target, me),
            device_id_type=MESH,
        )

    for chunk in range(CHUNKS):
        for i, offset in enumerate(offsets):
            target = peer(offset)
            for element in range(chunk * part, (chunk + 1) * part):
                pack_s[i, element] = pack(target, element)
            if chunk == 0 and i == 0:
                pl.semaphore_wait(
                    barrier, len(offsets) + has_prev.astype(jnp.int32) + has_next.astype(jnp.int32)
                )
            forward_copy(i, chunk).start()
    for element in range(rows):
        got_s[me, element] = pack(me, element)

    for fetch in fetches[1:]:
        fetch.wait()
    start = pl.multiple_of(me * rows, 8)
    area = jac_ref[pl.ds(start, rows), :] * lane_ref[2:3, 0:POINTS]
    weight_s[...] = jnp.zeros_like(weight_s)
    for i in range(4):
        weight_s[i, :, 0:POINTS] = geo_ref[i, pl.ds(start, rows), :] * area
    weight_s[4, :, 0:POINTS] = area

    for chunk in range(CHUNKS):
        for i in range(len(offsets)):
            forward_copy(i, chunk).wait_recv()
        span = slice(chunk * part, (chunk + 1) * part)
        x = jnp.concatenate(
            [got_s[source, element] for element in range(chunk * part, (chunk + 1) * part)
             for source in range(n_plane)], axis=0)
        energy_s[span, :] = jnp.sum((x * x).reshape(part, NZ, WIDE), axis=1)
        point_s[...] = dot3(x, ph_ref[...], pl_ref[...])
        if chunk == CHUNKS - 1:
            squares = energy_s[...]
            tail_energy = jnp.sum(squares * lane_ref[0:1, :], axis=1, keepdims=True)
            all_energy = jnp.sum(squares, axis=1, keepdims=True)
            log_share = jnp.log((tail_energy + energy_floor) / (all_energy + energy_floor))
            ramp = (log_share - sensor_centre) / sensor_width
            strength = svv_peak / (1.0 + jnp.exp(-ramp))
            strength_s[n_plane] = jnp.broadcast_to(strength, (rows, LANES))
            strength_s[me] = jnp.broadcast_to(strength, (rows, LANES))
            for i in range(len(offsets)):
                strength_copy(i).start()

        for local in range(part):
            element = chunk * part + local
            here = slice(local * NZ, (local + 1) * NZ)
            u = point_s[here, 0:LANES]
            v = point_s[here, LANES : 2 * LANES]
            w = point_s[here, 2 * LANES : 3 * LANES]
            g = [weight_s[i, element : element + 1, :] for i in range(5)]
            carriers = jnp.concatenate([g[0] * u + g[2] * v, g[1] * u + g[3] * v, g[4] * w], axis=1)
            speeds = dot(inv_ref[...], stacked_halves(carriers))
            slopes = dot(inv_ref[...], stacked_halves(point_s[here, 3 * LANES :]))
            along_z = dot(slo_ref[...], stacked_halves(point_s[here, 0 : 3 * LANES]))
            product = jnp.concatenate(
                [
                    speeds[:, 0:LANES] * slopes[:, f * LANES : (f + 1) * LANES]
                    + speeds[:, LANES : 2 * LANES] * slopes[:, (3 + f) * LANES : (4 + f) * LANES]
                    + speeds[:, 2 * LANES :] * along_z[:, f * LANES : (f + 1) * LANES]
                    for f in range(3)
                ],
                axis=1,
            )
            hat_s[here, :] = dot(fwd_ref[...], stacked_halves(product))
        weak = dot3(hat_s[...], mh_ref[...], ml_ref[...])
        for local in range(part):
            for k in range(n_plane):
                first = local * NZ + k * planes
                back_s[k, chunk * part + local] = weak[first : first + planes]
        for i in range(len(offsets)):
            back_copy(i, chunk).start()
        for local in range(part):
            weak_s[me, chunk * part + local] = back_s[me, chunk * part + local]

    for i in range(len(offsets)):
        strength_copy(i).wait_recv()
    for column in range(columns):
        factor = -strength_s[column] * lane_ref[1:2, 0:LANES]
        for field in range(3):
            for j in range(planes):
                at = slice(j * elements + column * rows, j * elements + (column + 1) * rows)
                svv_ref[field, at, :] = vel_ref[field, at, :] * factor[:, 0:MODES]

    for chunk in range(CHUNKS):
        for i in range(len(offsets)):
            back_copy(i, chunk).wait_recv()

    flipped = flip_ref[0] == 1
    turn = jnp.where(flipped, 1, 0)
    for i, column in ((0, 0), (1, columns - 1)):
        table = edge_ref[2 * i + turn]
        tiles = []
        for half in range(2):
            picked = jnp.concatenate([weak_s[column, 4 * half + s] for s in range(4)], axis=1)
            high, low = split(picked)
            tiles.append(dot(high, table) + dot(low, table))
        edge_out[i, 0] = jnp.where(flipped, tiles[1], tiles[0])
        edge_out[i, 1] = jnp.where(flipped, tiles[0], tiles[1])

    @pl.when(has_prev)
    def _():
        edge_copy(0, block - 1).start()

    @pl.when(has_next)
    def _():
        edge_copy(1, block + 1).start()

    wide = lax.broadcasted_iota(jnp.int32, (planes, WIDE), 1)
    side = P_SIZE + 1
    inside = wide < 3 * MODES
    is_left = inside & (lax.rem(wide, MODES) < side)
    is_right = inside & (lax.rem(wide, MODES) >= side) & (lax.rem(wide, MODES) < 2 * side)
    is_bottom = inside & (lax.rem(wide, side) == 0)
    is_top = inside & (lax.rem(wide, side) == 1)

    for row in range(rows):
        strip = [weak_s[column, row] for column in range(columns)]
        for column in range(columns):
            total = strip[column]
            if column > 0:
                total = total + jnp.where(is_left, pltpu.roll(strip[column - 1], WIDE - side, 1), 0.0)
            if column < columns - 1:
                total = total + jnp.where(is_right, pltpu.roll(strip[column + 1], side, 1), 0.0)
            got_s[column, row] = total

    @pl.when(has_next)
    def _():
        edge_copy(0, block + 1).wait_recv()

    @pl.when(block == n_elem - 1)
    def _():
        edge_in[0] = jnp.zeros((2, planes, LANES), jnp.float32)

    @pl.when(has_prev)
    def _():
        edge_copy(1, block - 1).wait_recv()

    @pl.when(block == 0)
    def _():
        edge_in[1] = jnp.zeros((2, planes, LANES), jnp.float32)

    for i, column in ((1, 0), (0, columns - 1)):
        table = edge_ref[2 * (1 - i) + turn]
        for half in range(2):
            tile = jnp.where(flipped, edge_in[i, 1 - half], edge_in[i, half])
            high, low = split(tile)
            spread = dot_t(high, table) + dot_t(low, table)
            for s in range(4):
                got_s[column, 4 * half + s] += spread[:, s * WIDE : (s + 1) * WIDE]

    for column in range(columns):
        strip = [got_s[column, row] for row in range(rows)]
        for row in range(rows):
            total = strip[row]
            if row > 0:
                total = total + jnp.where(is_bottom, pltpu.roll(strip[row - 1], WIDE - 1, 1), 0.0)
            if row < rows - 1:
                total = total + jnp.where(is_top, pltpu.roll(strip[row + 1], 1, 1), 0.0)
            fields = (
                total[:, 0:LANES],
                pltpu.roll(total, WIDE - MODES, 1)[:, 0:LANES],
                pltpu.roll(total, WIDE - 2 * MODES, 1)[:, 0:LANES],
            )
            for field in range(3):
                base = field * planes * elements + column * rows + row
                out_s[pl.ds(base, planes, stride=elements), :] = fields[field]
    for field in range(3):
        adv_ref[field] = out_s[field * planes * elements : (field + 1) * planes * elements, 0:MODES]

    for i in range(len(offsets)):
        strength_copy(i).wait_send()
        for chunk in range(CHUNKS):
            forward_copy(i, chunk).wait_send()
            back_copy(i, chunk).wait_send()

    @pl.when(has_prev)
    def _():
        edge_copy(0, block - 1).wait_send()

    @pl.when(has_next)
    def _():
        edge_copy(1, block + 1).wait_send()


def kernel_body(n_plane, n_elem, velocity, geometry, jacobian, frame_flip):
    planes, elements = velocity.shape[1], velocity.shape[3]
    tables = [jnp.asarray(table) for table in kernel_tables()]
    vel = velocity.transpose(0, 1, 3, 2).reshape(3, planes * elements, MODES)
    geo = geometry.transpose(0, 2, 1)
    jac = jacobian.transpose(1, 0)
    inputs = [vel, geo, jac, *tables]
    whole = pl.BlockSpec(memory_space=pltpu.VMEM)
    part = EY // CHUNKS
    flat = jax.ShapeDtypeStruct((3, planes * elements, MODES), jnp.float32)
    f32 = jnp.float32
    dma = pltpu.SemaphoreType.DMA
    others = n_plane - 1
    advection, svv = pl.pallas_call(
        functools.partial(advance, n_plane, n_elem),
        out_shape=(flat, flat),
        in_specs=[pl.BlockSpec(memory_space=pltpu.SMEM)] + [pl.BlockSpec(memory_space=pltpu.HBM)] * len(inputs),
        out_specs=(whole, whole),
        scratch_shapes=[pltpu.VMEM(x.shape, x.dtype) for x in inputs]
        + [
            pltpu.VMEM((3 * planes * elements, LANES), f32),
            pltpu.VMEM((others, EY, planes, WIDE), f32),
            pltpu.VMEM((n_plane, EY, planes, WIDE), f32),
            pltpu.VMEM((5, EY, LANES), f32),
            pltpu.VMEM((EY, WIDE), f32),
            pltpu.VMEM((n_plane + 1, EY, LANES), f32),
            pltpu.VMEM((part * NZ, 9 * LANES), f32),
            pltpu.VMEM((part * NZ, 3 * LANES), f32),
            pltpu.VMEM((n_plane, EY, planes, WIDE), f32),
            pltpu.VMEM((n_plane, EY, planes, WIDE), f32),
            pltpu.VMEM((2, 2, planes, LANES), f32),
            pltpu.VMEM((2, 2, planes, LANES), f32),
            pltpu.VMEM((3 * planes * elements, LANES), f32),
            dma((others, CHUNKS)),
            dma((others, CHUNKS)),
            dma((others,)),
            dma((others,)),
            dma((others, CHUNKS)),
            dma((others, CHUNKS)),
            dma((2,)),
            dma((2,)),
            dma((len(inputs),)),
        ],
        compiler_params=pltpu.CompilerParams(
            collective_id=0, has_side_effects=True, vmem_limit_bytes=40 * 1024 * 1024
        ),
    )(frame_flip, *inputs)

    def restore(x):
        return x.reshape(3, planes, elements, MODES).transpose(0, 1, 3, 2)

    return restore(advection), restore(svv)


def body(velocity, geometry, jacobian, frame_flip):
    value_table, xi_table, eta_table, point_weights, tail_mask, svv_weight, inverse, forward = (
        jnp.asarray(table.astype(np.float32)) for table in spectral_tables(P_SIZE, Q, NZ)
    )
    planes_here = velocity.shape[1]
    position = lax.axis_index("plane")
    wavenumbers = (position * (planes_here // 2) + jnp.arange(planes_here // 2)).astype(jnp.float32)
    zcoeffs = z_slope(velocity, wavenumbers)
    stacked = point_values(velocity, zcoeffs, geometry, value_table, xi_table, eta_table)
    gathered = to_points(stacked)
    nonlinear = advect(gathered, inverse, forward)
    returned = to_planes(nonlinear)
    weak_rhs = project(returned, jacobian, value_table, point_weights)
    tail_part, all_part = energies(velocity, tail_mask)
    tail_energy, all_energy = lax.psum((tail_part, all_part), "plane")
    strength = strength_ramp(tail_energy, all_energy)
    svv_force = -strength[None, None, None, :] * svv_weight[None, None, :, None] * velocity
    advection = assemble(weak_rhs, frame_flip[0])
    return (advection, svv_force)


def solution(mesh):
    n_plane, n_elem = mesh.shape["plane"], mesh.shape["elem"]
    fits = n_plane == 4 and (NZ // n_plane) % 16 == 0
    return jax.shard_map(
        functools.partial(kernel_body, n_plane, n_elem) if fits else body,
        mesh=mesh,
        in_specs=(
            P(None, "plane", None, "elem"),
            P(None, None, "elem"),
            P(None, "elem"),
            P("elem"),
        ),
        out_specs=(P(None, "plane", None, "elem"), P(None, "plane", None, "elem")),
        check_vma=False,
    )
```

```python
import functools

import jax
import jax.numpy as jnp
import numpy as np
from jax import lax
from jax.experimental import pallas as pl
from jax.experimental.pallas import tpu as pltpu
from jax.sharding import PartitionSpec as P

P_SIZE = 8
Q = 10
NZ = 64
EY = 8


spanwise_scale = 0.25
svv_cutoff = 4.0
svv_peak = 2.0
sensor_centre = -1.5
sensor_width = 0.6
energy_floor = 1e-06


def from_behind(block, axis, distance):
    devices = range(lax.axis_size(axis))
    route = [(i - distance, i) for i in devices if i - distance in devices]
    return lax.ppermute(block, axis, route)


def modal_basis(top_degree, points):
    legendre = [points * 0.0 + 1.0, points * 1.0]
    for order in range(1, top_degree):
        legendre.append(
            ((2.0 * order + 1.0) * points * legendre[order] - order * legendre[order - 1])
            / (order + 1.0)
        )
    values = np.zeros((points.shape[0], top_degree + 1))
    slopes = np.zeros((points.shape[0], top_degree + 1))
    values[:, 0] = 0.5 * (1.0 - points)
    values[:, 1] = 0.5 * (1.0 + points)
    slopes[:, 0] = -0.5
    slopes[:, 1] = 0.5
    for column in range(2, top_degree + 1):
        values[:, column] = (legendre[column - 2] - points * legendre[column - 1]) / column
        slopes[:, column] = -legendre[column - 1]
    return (values, slopes)


def spectral_tables(top_degree, point_count, planes):
    fine_planes = 3 * planes // 2
    angles_q = np.pi * (np.arange(point_count) + 0.5) / point_count
    points = -np.cos(angles_q)
    series = np.arange(1, point_count // 2 + 1)
    weights = (
        2.0
        / point_count
        * (
            1.0
            - 2.0
            * np.sum(
                np.cos(2.0 * series[None, :] * angles_q[:, None])
                / (4.0 * series[None, :] ** 2 - 1.0),
                axis=1,
            )
        )
    )
    values, slopes = modal_basis(top_degree, points)
    value_table = np.kron(values, values)
    xi_table = np.kron(slopes, values)
    eta_table = np.kron(values, slopes)
    point_weights = np.kron(weights, weights)
    degrees = np.maximum(np.arange(top_degree + 1), 1) * 1.0
    highest = np.maximum(degrees[:, None], degrees[None, :]).reshape(-1)
    tail_mask = (highest > svv_cutoff) * 1.0
    kernel = np.where(
        degrees > svv_cutoff,
        np.exp(-(((top_degree - degrees) / np.maximum(degrees - svv_cutoff, 1.0)) ** 2)),
        0.0,
    )
    per_dir = degrees * (degrees + 1.0) * kernel
    svv_weight = (per_dir[:, None] + per_dir[None, :]).reshape(-1) / (
        top_degree * (top_degree + 1.0)
    )
    angles_z = 2.0 * np.pi * np.arange(fine_planes) / fine_planes
    coef_index = np.arange(planes)
    wavenumber = np.where(coef_index == 1, planes // 2, coef_index // 2)
    cosine_part = (coef_index % 2 == 0) | (coef_index == 1)
    inverse = np.where(
        cosine_part[None, :],
        np.cos(wavenumber[None, :] * angles_z[:, None]),
        np.sin(wavenumber[None, :] * angles_z[:, None]),
    )
    forward = inverse.T * np.where(coef_index == 0, 1.0 / fine_planes, 2.0 / fine_planes)[:, None]
    return (
        value_table,
        xi_table,
        eta_table,
        point_weights,
        tail_mask,
        svv_weight,
        inverse,
        forward,
    )


def z_slope(coeffs, wavenumbers):
    fields, planes, mode_count, elements = coeffs.shape
    paired = coeffs.reshape(fields, planes // 2, 2, mode_count, elements)
    factor = (spanwise_scale * wavenumbers)[None, :, None, None]
    slope = jnp.stack([factor * paired[:, :, 1], -factor * paired[:, :, 0]], axis=2)
    return slope.reshape(coeffs.shape)


def point_values(coeffs, zcoeffs, geometry, value_table, xi_table, eta_table):
    highest = lax.Precision.HIGHEST
    values = jnp.einsum("qm,fjme->fjqe", value_table, coeffs, precision=highest)
    along_xi = jnp.einsum("qm,fjme->fjqe", xi_table, coeffs, precision=highest)
    along_eta = jnp.einsum("qm,fjme->fjqe", eta_table, coeffs, precision=highest)
    along_z = jnp.einsum("qm,fjme->fjqe", value_table, zcoeffs, precision=highest)
    slope_x = geometry[0] * along_xi + geometry[1] * along_eta
    slope_y = geometry[2] * along_xi + geometry[3] * along_eta
    return jnp.concatenate([values, slope_x, slope_y, along_z], axis=0)


def advect(stacked, inverse, forward):
    highest = lax.Precision.HIGHEST
    physical = jnp.einsum("nj,cjqe->cnqe", inverse, stacked, precision=highest)
    speeds = physical[0:3]
    product = speeds[0] * physical[3:6] + speeds[1] * physical[6:9] + speeds[2] * physical[9:12]
    return jnp.einsum("jn,fnqe->fjqe", forward, product, precision=highest)


def project(nonlinear, jacobian, value_table, point_weights):
    weighted = nonlinear * (jacobian * point_weights[:, None])
    return jnp.einsum("qm,fjqe->fjme", value_table, weighted, precision=lax.Precision.HIGHEST)


def energies(coeffs, tail_mask):
    squares = coeffs * coeffs
    tail_energy = jnp.sum(squares * tail_mask[:, None], axis=(0, 1, 2))
    all_energy = jnp.sum(squares, axis=(0, 1, 2))
    return (tail_energy, all_energy)


def strength_ramp(tail_energy, all_energy):
    log_share = jnp.log((tail_energy + energy_floor) / (all_energy + energy_floor))
    return svv_peak * jax.nn.sigmoid((log_share - sensor_centre) / sensor_width)


def flip_edge(edge_modes):
    count_r = edge_modes.shape[2]
    parity = jnp.where(jnp.arange(2, count_r) % 2 == 0, 1.0, -1.0).astype(jnp.float32)
    parity = parity.reshape((-1,) + (1,) * (edge_modes.ndim - 3))
    swapped = jnp.concatenate(
        [edge_modes[:, :, 1:2], edge_modes[:, :, 0:1], edge_modes[:, :, 2:] * parity], axis=2
    )
    return jnp.flip(swapped, axis=-1)


def to_points(stacked):
    return lax.all_to_all(stacked, "plane", split_axis=3, concat_axis=1, tiled=True)


def to_planes(returned):
    return lax.all_to_all(returned, "plane", split_axis=1, concat_axis=3, tiled=True)


def assemble(weak_rhs, flip_flag):
    fields, planes, mode_count, elements = weak_rhs.shape
    side = P_SIZE + 1
    columns = elements // EY
    modal_grid = weak_rhs.reshape(fields, planes, side, side, columns, EY)
    left_modes = modal_grid[:, :, 0]
    right_modes = modal_grid[:, :, 1]
    flipped = flip_flag == 1

    def canonical(edge_modes):
        return jnp.where(flipped, flip_edge(edge_modes), edge_modes)

    out_right = canonical(right_modes[:, :, :, -1])
    out_left = canonical(left_modes[:, :, :, 0])
    from_left = canonical(from_behind(out_right, "elem", 1))
    from_right = canonical(from_behind(out_left, "elem", -1))
    left_next = jnp.concatenate([left_modes[:, :, :, 1:], from_right[:, :, :, None]], axis=3)
    right_prev = jnp.concatenate([from_left[:, :, :, None], right_modes[:, :, :, :-1]], axis=3)
    modal_grid = jnp.concatenate(
        [
            (left_modes + right_prev)[:, :, None],
            (right_modes + left_next)[:, :, None],
            modal_grid[:, :, 2:],
        ],
        axis=2,
    )
    bottom = modal_grid[:, :, :, 0]
    top = modal_grid[:, :, :, 1]
    no_row = jnp.zeros_like(bottom[..., :1])
    new_bottom = bottom + jnp.concatenate([no_row, top[..., :-1]], axis=-1)
    new_top = top + jnp.concatenate([bottom[..., 1:], no_row], axis=-1)
    modal_grid = jnp.concatenate(
        [new_bottom[:, :, :, None], new_top[:, :, :, None], modal_grid[:, :, :, 2:]], axis=3
    )
    return modal_grid.reshape(weak_rhs.shape)


MODES = (P_SIZE + 1) * (P_SIZE + 1)
POINTS = Q * Q
FINE = 3 * NZ // 2
WIDE = 256
LANES = 128
CHUNKS = 4
TABLES = 9
MESH = pl.DeviceIdType.MESH


def halves(table):
    high = table.astype(np.float32).astype(jnp.bfloat16)
    low = (table - high.astype(np.float64)).astype(jnp.bfloat16)
    return high, low


def kernel_tables():
    value, xi, eta, weights, tail, svv, inverse, forward = spectral_tables(P_SIZE, Q, NZ)
    to_point = np.zeros((WIDE, 9 * LANES))
    to_mode = np.zeros((3 * LANES, WIDE))
    for field in range(3):
        rows = slice(field * MODES, (field + 1) * MODES)
        for kind, table in enumerate((value, xi, eta)):
            start = (kind * 3 + field) * LANES
            to_point[rows, start : start + POINTS] = table.T
        to_mode[field * LANES : field * LANES + POINTS, rows] = value
    slope = np.zeros((FINE, NZ))
    for m in range(1, NZ // 2):
        slope[:, 2 * m + 1] = spanwise_scale * m * inverse[:, 2 * m]
        slope[:, 2 * m] = -spanwise_scale * m * inverse[:, 2 * m + 1]

    def triple(table):
        high, low = halves(table)
        return np.concatenate([high, low, high], axis=1)

    lanes = np.zeros((8, WIDE), np.float32)
    lanes[0, : 3 * MODES] = np.tile(tail, 3)
    lanes[1, :MODES] = svv
    lanes[2, :POINTS] = weights
    edges = np.zeros((2, 2, 4, WIDE, LANES), np.float32)
    side = P_SIZE + 1
    for end in range(2):
        for slot in range(4):
            for field in range(3):
                for r in range(side):
                    source = field * MODES + end * side
                    edges[end, 0, slot, source + r, slot * 32 + field * side + r] = 1.0
                    swapped = 1 - r if r < 2 else r
                    sign = 1.0 if r < 2 or r % 2 == 0 else -1.0
                    edges[end, 1, slot, source + swapped, (3 - slot) * 32 + field * side + r] = sign
    edges = edges.reshape(4, 4 * WIDE, LANES).astype(jnp.bfloat16)
    return (
        lanes,
        *halves(to_point),
        triple(inverse),
        triple(slope),
        triple(forward),
        *halves(to_mode),
        edges,
    )


def split(x):
    high = x.astype(jnp.bfloat16)
    return high, (x - high.astype(jnp.float32)).astype(jnp.bfloat16)


def dot(a, b):
    return lax.dot_general(a, b, (((1,), (0,)), ((), ())), preferred_element_type=jnp.float32)


def dot_t(a, b):
    return lax.dot_general(a, b, (((1,), (1,)), ((), ())), preferred_element_type=jnp.float32)


def dot3(x, high, low):
    x_high, x_low = split(x)
    return dot(x_high, high) + dot(x_high, low) + dot(x_low, high)


def stacked_halves(x):
    high, low = split(x)
    return jnp.concatenate([high, high, low], axis=0)


def advance(n_plane, n_elem, flip_ref, *refs):
    n_in = 3 + TABLES
    sources, (joined_ref, sense_ref), held = refs[:n_in], refs[n_in : n_in + 2], refs[n_in + 2 : 2 * n_in + 2]
    fetches = [
        pltpu.make_async_copy(source, target, refs[-1].at[i])
        for i, (source, target) in enumerate(zip(sources, held))
    ]
    for fetch in fetches:
        fetch.start()
    advance_block(n_plane, n_elem, fetches, flip_ref, *held, joined_ref, sense_ref, *refs[2 * n_in + 2 : -1])


def advance_block(n_plane, n_elem, fetches, flip_ref, vel_ref, geo_ref, jac_ref, lane_ref, ph_ref,
            pl_ref, inv_ref, slo_ref, fwd_ref, mh_ref, ml_ref, edge_ref, joined_ref, sense_ref,
            vel_s, pack_s, got_s, weight_s, energy_s, strength_s, point_s, hat_s, back_s, weak_s,
            edge_out, edge_in,
            send_a, recv_a, send_s, recv_s, send_b, recv_b, send_e, recv_e):
    block = lax.axis_index("elem")
    me = lax.axis_index("plane")
    planes = NZ // n_plane
    rows = EY
    columns = n_plane
    elements = rows * columns
    part = rows // CHUNKS
    offsets = [2, 1, 3]
    has_prev = block > 0
    has_next = block < n_elem - 1

    def peer(offset):
        return lax.rem(me + offset, n_plane)

    barrier = pltpu.get_barrier_semaphore()
    for offset in offsets:
        pl.semaphore_signal(barrier, inc=1, device_id=(block, peer(offset)), device_id_type=MESH)

    @pl.when(has_prev)
    def _():
        pl.semaphore_signal(barrier, inc=1, device_id=(block - 1, me), device_id_type=MESH)

    @pl.when(has_next)
    def _():
        pl.semaphore_signal(barrier, inc=1, device_id=(block + 1, me), device_id_type=MESH)

    fetches[0].wait()
    for field in range(3):
        vel_s[field * planes * elements : (field + 1) * planes * elements, 0:MODES] = vel_ref[field]

    lane = lax.broadcasted_iota(jnp.int32, (planes, LANES), 1)
    first_cut = LANES - MODES

    def pack(target, element):
        base = target * rows + element
        u, v, w = [
            vel_s[pl.ds(field * planes * elements + base, planes, stride=elements), :]
            for field in range(3)
        ]
        v_turned = pltpu.roll(v, MODES, 1)
        w_turned = pltpu.roll(w, 2 * MODES - LANES, 1)
        left = jnp.where(lane < MODES, u, v_turned)
        right = jnp.where(
            lane < 2 * MODES - LANES, v_turned, jnp.where(lane < 3 * MODES - LANES, w_turned, 0.0)
        )
        return jnp.concatenate([left, right], axis=1)

    def forward_copy(i, chunk):
        span = pl.ds(chunk * part, part)
        return pltpu.make_async_remote_copy(
            src_ref=pack_s.at[i, span],
            dst_ref=got_s.at[me, span],
            send_sem=send_a.at[i, chunk],
            recv_sem=recv_a.at[i, chunk],
            device_id=(block, peer(offsets[i])),
            device_id_type=MESH,
        )

    def back_copy(i, chunk):
        span = pl.ds(chunk * part, part)
        return pltpu.make_async_remote_copy(
            src_ref=back_s.at[peer(offsets[i]), span],
            dst_ref=weak_s.at[me, span],
            send_sem=send_b.at[i, chunk],
            recv_sem=recv_b.at[i, chunk],
            device_id=(block, peer(offsets[i])),
            device_id_type=MESH,
        )

    def strength_copy(i):
        return pltpu.make_async_remote_copy(
            src_ref=strength_s.at[n_plane],
            dst_ref=strength_s.at[me],
            send_sem=send_s.at[i],
            recv_sem=recv_s.at[i],
            device_id=(block, peer(offsets[i])),
            device_id_type=MESH,
        )

    def edge_copy(i, target):
        return pltpu.make_async_remote_copy(
            src_ref=edge_out.at[i],
            dst_ref=edge_in.at[i],
            send_sem=send_e.at[i],
            recv_sem=recv_e.at[i],
            device_id=(target, me),
            device_id_type=MESH,
        )

    for chunk in range(CHUNKS):
        for i, offset in enumerate(offsets):
            target = peer(offset)
            for element in range(chunk * part, (chunk + 1) * part):
                pack_s[i, element] = pack(target, element)
            if chunk == 0 and i == 0:
                pl.semaphore_wait(
                    barrier, len(offsets) + has_prev.astype(jnp.int32) + has_next.astype(jnp.int32)
                )
            forward_copy(i, chunk).start()
    for element in range(rows):
        got_s[me, element] = pack(me, element)

    for fetch in fetches[1:]:
        fetch.wait()
    start = pl.multiple_of(me * rows, 8)
    area = jac_ref[pl.ds(start, rows), :] * lane_ref[2:3, 0:POINTS]
    weight_s[...] = jnp.zeros_like(weight_s)
    for i in range(4):
        weight_s[i, :, 0:POINTS] = geo_ref[i, pl.ds(start, rows), :] * area
    weight_s[4, :, 0:POINTS] = area

    for chunk in range(CHUNKS):
        for i in range(len(offsets)):
            forward_copy(i, chunk).wait_recv()
        span = slice(chunk * part, (chunk + 1) * part)
        x = jnp.concatenate(
            [got_s[source, element] for element in range(chunk * part, (chunk + 1) * part)
             for source in range(n_plane)], axis=0)
        energy_s[span, :] = jnp.sum((x * x).reshape(part, NZ, WIDE), axis=1)
        point_s[...] = dot3(x, ph_ref[...], pl_ref[...])
        if chunk == CHUNKS - 1:
            squares = energy_s[...]
            tail_energy = jnp.sum(squares * lane_ref[0:1, :], axis=1, keepdims=True)
            all_energy = jnp.sum(squares, axis=1, keepdims=True)
            log_share = jnp.log((tail_energy + energy_floor) / (all_energy + energy_floor))
            ramp = (log_share - sensor_centre) / sensor_width
            strength = svv_peak / (1.0 + jnp.exp(-ramp))
            strength_s[n_plane] = jnp.broadcast_to(strength, (rows, LANES))
            strength_s[me] = jnp.broadcast_to(strength, (rows, LANES))
            for i in range(len(offsets)):
                strength_copy(i).start()

        for local in range(part):
            element = chunk * part + local
            here = slice(local * NZ, (local + 1) * NZ)
            u = point_s[here, 0:LANES]
            v = point_s[here, LANES : 2 * LANES]
            w = point_s[here, 2 * LANES : 3 * LANES]
            g = [weight_s[i, element : element + 1, :] for i in range(5)]
            carriers = jnp.concatenate([g[0] * u + g[2] * v, g[1] * u + g[3] * v, g[4] * w], axis=1)
            speeds = dot(inv_ref[...], stacked_halves(carriers))
            slopes = dot(inv_ref[...], stacked_halves(point_s[here, 3 * LANES :]))
            along_z = dot(slo_ref[...], stacked_halves(point_s[here, 0 : 3 * LANES]))
            product = jnp.concatenate(
                [
                    speeds[:, 0:LANES] * slopes[:, f * LANES : (f + 1) * LANES]
                    + speeds[:, LANES : 2 * LANES] * slopes[:, (3 + f) * LANES : (4 + f) * LANES]
                    + speeds[:, 2 * LANES :] * along_z[:, f * LANES : (f + 1) * LANES]
                    for f in range(3)
                ],
                axis=1,
            )
            hat_s[here, :] = dot(fwd_ref[...], stacked_halves(product))
        weak = dot3(hat_s[...], mh_ref[...], ml_ref[...])
        for local in range(part):
            for k in range(n_plane):
                first = local * NZ + k * planes
                back_s[k, chunk * part + local] = weak[first : first + planes]
        for i in range(len(offsets)):
            back_copy(i, chunk).start()
        for local in range(part):
            weak_s[me, chunk * part + local] = back_s[me, chunk * part + local]

    for i in range(len(offsets)):
        strength_copy(i).wait_recv()
    sense_ref[...] = strength_s[0:n_plane]

    for chunk in range(CHUNKS):
        for i in range(len(offsets)):
            back_copy(i, chunk).wait_recv()

    flipped = flip_ref[0] == 1
    turn = jnp.where(flipped, 1, 0)
    for i, column in ((0, 0), (1, columns - 1)):
        table = edge_ref[2 * i + turn]
        tiles = []
        for half in range(2):
            picked = jnp.concatenate([weak_s[column, 4 * half + s] for s in range(4)], axis=1)
            high, low = split(picked)
            tiles.append(dot(high, table) + dot(low, table))
        edge_out[i, 0] = jnp.where(flipped, tiles[1], tiles[0])
        edge_out[i, 1] = jnp.where(flipped, tiles[0], tiles[1])

    @pl.when(has_prev)
    def _():
        edge_copy(0, block - 1).start()

    @pl.when(has_next)
    def _():
        edge_copy(1, block + 1).start()

    wide = lax.broadcasted_iota(jnp.int32, (planes, WIDE), 1)
    side = P_SIZE + 1
    inside = wide < 3 * MODES
    is_left = inside & (lax.rem(wide, MODES) < side)
    is_right = inside & (lax.rem(wide, MODES) >= side) & (lax.rem(wide, MODES) < 2 * side)

    for row in range(rows):
        strip = [weak_s[column, row] for column in range(columns)]
        for column in range(columns):
            total = strip[column]
            if column > 0:
                total = total + jnp.where(is_left, pltpu.roll(strip[column - 1], WIDE - side, 1), 0.0)
            if column < columns - 1:
                total = total + jnp.where(is_right, pltpu.roll(strip[column + 1], side, 1), 0.0)
            got_s[column, row] = total

    @pl.when(has_next)
    def _():
        edge_copy(0, block + 1).wait_recv()

    @pl.when(block == n_elem - 1)
    def _():
        edge_in[0] = jnp.zeros((2, planes, LANES), jnp.float32)

    @pl.when(has_prev)
    def _():
        edge_copy(1, block - 1).wait_recv()

    @pl.when(block == 0)
    def _():
        edge_in[1] = jnp.zeros((2, planes, LANES), jnp.float32)

    for i, column in ((1, 0), (0, columns - 1)):
        table = edge_ref[2 * (1 - i) + turn]
        for half in range(2):
            tile = jnp.where(flipped, edge_in[i, 1 - half], edge_in[i, half])
            high, low = split(tile)
            spread = dot_t(high, table) + dot_t(low, table)
            for s in range(4):
                got_s[column, 4 * half + s] += spread[:, s * WIDE : (s + 1) * WIDE]

    joined_ref[...] = got_s[...]

    for i in range(len(offsets)):
        strength_copy(i).wait_send()
        for chunk in range(CHUNKS):
            forward_copy(i, chunk).wait_send()
            back_copy(i, chunk).wait_send()

    @pl.when(has_prev)
    def _():
        edge_copy(0, block - 1).wait_send()

    @pl.when(has_next)
    def _():
        edge_copy(1, block + 1).wait_send()


def finish(joined_ref, sense_ref, vel_ref, lane_ref, adv_ref, svv_ref, out_s):
    planes = joined_ref.shape[2]
    side = P_SIZE + 1
    wide = lax.broadcasted_iota(jnp.int32, (planes, WIDE), 1)
    inside = wide < 3 * MODES
    is_bottom = inside & (lax.rem(wide, side) == 0)
    is_top = inside & (lax.rem(wide, side) == 1)
    factor = -sense_ref[0] * lane_ref[1:2, 0:LANES]
    svv_ref[...] = vel_ref[...] * factor[:, 0:MODES]
    strip = [joined_ref[0, row] for row in range(EY)]
    for row in range(EY):
        total = strip[row]
        if row > 0:
            total = total + jnp.where(is_bottom, pltpu.roll(strip[row - 1], WIDE - 1, 1), 0.0)
        if row < EY - 1:
            total = total + jnp.where(is_top, pltpu.roll(strip[row + 1], 1, 1), 0.0)
        fields = (
            total[:, 0:LANES],
            pltpu.roll(total, WIDE - MODES, 1)[:, 0:LANES],
            pltpu.roll(total, WIDE - 2 * MODES, 1)[:, 0:LANES],
        )
        for field in range(3):
            out_s[pl.ds(field * planes * EY + row, planes, stride=EY), :] = fields[field]
    for field in range(3):
        block = out_s[field * planes * EY : (field + 1) * planes * EY, 0:MODES]
        adv_ref[field] = block.reshape(planes, EY, MODES)


def kernel_body(n_plane, n_elem, velocity, geometry, jacobian, frame_flip):
    planes, elements = velocity.shape[1], velocity.shape[3]
    tables = [jnp.asarray(table) for table in kernel_tables()]
    vel = velocity.transpose(0, 1, 3, 2).reshape(3, planes * elements, MODES)
    geo = geometry.transpose(0, 2, 1)
    jac = jacobian.transpose(1, 0)
    inputs = [vel, geo, jac, *tables]
    whole = pl.BlockSpec(memory_space=pltpu.VMEM)
    part = EY // CHUNKS
    f32 = jnp.float32
    dma = pltpu.SemaphoreType.DMA
    others = n_plane - 1
    joined, sense = pl.pallas_call(
        functools.partial(advance, n_plane, n_elem),
        out_shape=(
            jax.ShapeDtypeStruct((n_plane, EY, planes, WIDE), f32),
            jax.ShapeDtypeStruct((n_plane, EY, LANES), f32),
        ),
        in_specs=[pl.BlockSpec(memory_space=pltpu.SMEM)] + [pl.BlockSpec(memory_space=pltpu.HBM)] * len(inputs),
        out_specs=(whole, whole),
        scratch_shapes=[pltpu.VMEM(x.shape, x.dtype) for x in inputs]
        + [
            pltpu.VMEM((3 * planes * elements, LANES), f32),
            pltpu.VMEM((others, EY, planes, WIDE), f32),
            pltpu.VMEM((n_plane, EY, planes, WIDE), f32),
            pltpu.VMEM((5, EY, LANES), f32),
            pltpu.VMEM((EY, WIDE), f32),
            pltpu.VMEM((n_plane + 1, EY, LANES), f32),
            pltpu.VMEM((part * NZ, 9 * LANES), f32),
            pltpu.VMEM((part * NZ, 3 * LANES), f32),
            pltpu.VMEM((n_plane, EY, planes, WIDE), f32),
            pltpu.VMEM((n_plane, EY, planes, WIDE), f32),
            pltpu.VMEM((2, 2, planes, LANES), f32),
            pltpu.VMEM((2, 2, planes, LANES), f32),
            dma((others, CHUNKS)),
            dma((others, CHUNKS)),
            dma((others,)),
            dma((others,)),
            dma((others, CHUNKS)),
            dma((others, CHUNKS)),
            dma((2,)),
            dma((2,)),
            dma((len(inputs),)),
        ],
        compiler_params=pltpu.CompilerParams(
            collective_id=0, has_side_effects=True, vmem_limit_bytes=61 * 1024 * 1024
        ),
    )(frame_flip, *inputs)

    slab = pl.BlockSpec((3, planes, EY, MODES), lambda c: (0, 0, c, 0))
    full = jax.ShapeDtypeStruct((3, planes, elements, MODES), f32)
    advection, svv = pl.pallas_call(
        finish,
        out_shape=(full, full),
        grid=(n_plane,),
        in_specs=[
            pl.BlockSpec((1, EY, planes, WIDE), lambda c: (c, 0, 0, 0)),
            pl.BlockSpec((1, EY, LANES), lambda c: (c, 0, 0)),
            slab,
            pl.BlockSpec((8, WIDE), lambda c: (0, 0)),
        ],
        out_specs=(slab, slab),
        scratch_shapes=[pltpu.VMEM((3 * planes * EY, LANES), f32)],
        compiler_params=pltpu.CompilerParams(vmem_limit_bytes=61 * 1024 * 1024),
    )(joined, sense, velocity.transpose(0, 1, 3, 2), tables[0])
    return advection.transpose(0, 1, 3, 2), svv.transpose(0, 1, 3, 2)


def body(velocity, geometry, jacobian, frame_flip):
    value_table, xi_table, eta_table, point_weights, tail_mask, svv_weight, inverse, forward = (
        jnp.asarray(table.astype(np.float32)) for table in spectral_tables(P_SIZE, Q, NZ)
    )
    planes_here = velocity.shape[1]
    position = lax.axis_index("plane")
    wavenumbers = (position * (planes_here // 2) + jnp.arange(planes_here // 2)).astype(jnp.float32)
    zcoeffs = z_slope(velocity, wavenumbers)
    stacked = point_values(velocity, zcoeffs, geometry, value_table, xi_table, eta_table)
    gathered = to_points(stacked)
    nonlinear = advect(gathered, inverse, forward)
    returned = to_planes(nonlinear)
    weak_rhs = project(returned, jacobian, value_table, point_weights)
    tail_part, all_part = energies(velocity, tail_mask)
    tail_energy, all_energy = lax.psum((tail_part, all_part), "plane")
    strength = strength_ramp(tail_energy, all_energy)
    svv_force = -strength[None, None, None, :] * svv_weight[None, None, :, None] * velocity
    advection = assemble(weak_rhs, frame_flip[0])
    return (advection, svv_force)


def solution(mesh):
    n_plane, n_elem = mesh.shape["plane"], mesh.shape["elem"]
    fits = n_plane == 4 and (NZ // n_plane) % 16 == 0
    return jax.shard_map(
        functools.partial(kernel_body, n_plane, n_elem) if fits else body,
        mesh=mesh,
        in_specs=(
            P(None, "plane", None, "elem"),
            P(None, None, "elem"),
            P(None, "elem"),
            P("elem"),
        ),
        out_specs=(P(None, "plane", None, "elem"), P(None, "plane", None, "elem")),
        check_vma=False,
    )
```

```python
import functools

import jax
import jax.numpy as jnp
import numpy as np
from jax import lax
from jax.experimental import pallas as pl
from jax.experimental.pallas import tpu as pltpu
from jax.sharding import PartitionSpec as P

P_SIZE = 8
Q = 10
NZ = 64
EY = 8


spanwise_scale = 0.25
svv_cutoff = 4.0
svv_peak = 2.0
sensor_centre = -1.5
sensor_width = 0.6
energy_floor = 1e-06


def from_behind(block, axis, distance):
    devices = range(lax.axis_size(axis))
    route = [(i - distance, i) for i in devices if i - distance in devices]
    return lax.ppermute(block, axis, route)


def modal_basis(top_degree, points):
    legendre = [points * 0.0 + 1.0, points * 1.0]
    for order in range(1, top_degree):
        legendre.append(
            ((2.0 * order + 1.0) * points * legendre[order] - order * legendre[order - 1])
            / (order + 1.0)
        )
    values = np.zeros((points.shape[0], top_degree + 1))
    slopes = np.zeros((points.shape[0], top_degree + 1))
    values[:, 0] = 0.5 * (1.0 - points)
    values[:, 1] = 0.5 * (1.0 + points)
    slopes[:, 0] = -0.5
    slopes[:, 1] = 0.5
    for column in range(2, top_degree + 1):
        values[:, column] = (legendre[column - 2] - points * legendre[column - 1]) / column
        slopes[:, column] = -legendre[column - 1]
    return (values, slopes)


def spectral_tables(top_degree, point_count, planes):
    fine_planes = 3 * planes // 2
    angles_q = np.pi * (np.arange(point_count) + 0.5) / point_count
    points = -np.cos(angles_q)
    series = np.arange(1, point_count // 2 + 1)
    weights = (
        2.0
        / point_count
        * (
            1.0
            - 2.0
            * np.sum(
                np.cos(2.0 * series[None, :] * angles_q[:, None])
                / (4.0 * series[None, :] ** 2 - 1.0),
                axis=1,
            )
        )
    )
    values, slopes = modal_basis(top_degree, points)
    value_table = np.kron(values, values)
    xi_table = np.kron(slopes, values)
    eta_table = np.kron(values, slopes)
    point_weights = np.kron(weights, weights)
    degrees = np.maximum(np.arange(top_degree + 1), 1) * 1.0
    highest = np.maximum(degrees[:, None], degrees[None, :]).reshape(-1)
    tail_mask = (highest > svv_cutoff) * 1.0
    kernel = np.where(
        degrees > svv_cutoff,
        np.exp(-(((top_degree - degrees) / np.maximum(degrees - svv_cutoff, 1.0)) ** 2)),
        0.0,
    )
    per_dir = degrees * (degrees + 1.0) * kernel
    svv_weight = (per_dir[:, None] + per_dir[None, :]).reshape(-1) / (
        top_degree * (top_degree + 1.0)
    )
    angles_z = 2.0 * np.pi * np.arange(fine_planes) / fine_planes
    coef_index = np.arange(planes)
    wavenumber = np.where(coef_index == 1, planes // 2, coef_index // 2)
    cosine_part = (coef_index % 2 == 0) | (coef_index == 1)
    inverse = np.where(
        cosine_part[None, :],
        np.cos(wavenumber[None, :] * angles_z[:, None]),
        np.sin(wavenumber[None, :] * angles_z[:, None]),
    )
    forward = inverse.T * np.where(coef_index == 0, 1.0 / fine_planes, 2.0 / fine_planes)[:, None]
    return (
        value_table,
        xi_table,
        eta_table,
        point_weights,
        tail_mask,
        svv_weight,
        inverse,
        forward,
    )


def z_slope(coeffs, wavenumbers):
    fields, planes, mode_count, elements = coeffs.shape
    paired = coeffs.reshape(fields, planes // 2, 2, mode_count, elements)
    factor = (spanwise_scale * wavenumbers)[None, :, None, None]
    slope = jnp.stack([factor * paired[:, :, 1], -factor * paired[:, :, 0]], axis=2)
    return slope.reshape(coeffs.shape)


def point_values(coeffs, zcoeffs, geometry, value_table, xi_table, eta_table):
    highest = lax.Precision.HIGHEST
    values = jnp.einsum("qm,fjme->fjqe", value_table, coeffs, precision=highest)
    along_xi = jnp.einsum("qm,fjme->fjqe", xi_table, coeffs, precision=highest)
    along_eta = jnp.einsum("qm,fjme->fjqe", eta_table, coeffs, precision=highest)
    along_z = jnp.einsum("qm,fjme->fjqe", value_table, zcoeffs, precision=highest)
    slope_x = geometry[0] * along_xi + geometry[1] * along_eta
    slope_y = geometry[2] * along_xi + geometry[3] * along_eta
    return jnp.concatenate([values, slope_x, slope_y, along_z], axis=0)


def advect(stacked, inverse, forward):
    highest = lax.Precision.HIGHEST
    physical = jnp.einsum("nj,cjqe->cnqe", inverse, stacked, precision=highest)
    speeds = physical[0:3]
    product = speeds[0] * physical[3:6] + speeds[1] * physical[6:9] + speeds[2] * physical[9:12]
    return jnp.einsum("jn,fnqe->fjqe", forward, product, precision=highest)


def project(nonlinear, jacobian, value_table, point_weights):
    weighted = nonlinear * (jacobian * point_weights[:, None])
    return jnp.einsum("qm,fjqe->fjme", value_table, weighted, precision=lax.Precision.HIGHEST)


def energies(coeffs, tail_mask):
    squares = coeffs * coeffs
    tail_energy = jnp.sum(squares * tail_mask[:, None], axis=(0, 1, 2))
    all_energy = jnp.sum(squares, axis=(0, 1, 2))
    return (tail_energy, all_energy)


def strength_ramp(tail_energy, all_energy):
    log_share = jnp.log((tail_energy + energy_floor) / (all_energy + energy_floor))
    return svv_peak * jax.nn.sigmoid((log_share - sensor_centre) / sensor_width)


def flip_edge(edge_modes):
    count_r = edge_modes.shape[2]
    parity = jnp.where(jnp.arange(2, count_r) % 2 == 0, 1.0, -1.0).astype(jnp.float32)
    parity = parity.reshape((-1,) + (1,) * (edge_modes.ndim - 3))
    swapped = jnp.concatenate(
        [edge_modes[:, :, 1:2], edge_modes[:, :, 0:1], edge_modes[:, :, 2:] * parity], axis=2
    )
    return jnp.flip(swapped, axis=-1)


def to_points(stacked):
    return lax.all_to_all(stacked, "plane", split_axis=3, concat_axis=1, tiled=True)


def to_planes(returned):
    return lax.all_to_all(returned, "plane", split_axis=1, concat_axis=3, tiled=True)


def assemble(weak_rhs, flip_flag):
    fields, planes, mode_count, elements = weak_rhs.shape
    side = P_SIZE + 1
    columns = elements // EY
    modal_grid = weak_rhs.reshape(fields, planes, side, side, columns, EY)
    left_modes = modal_grid[:, :, 0]
    right_modes = modal_grid[:, :, 1]
    flipped = flip_flag == 1

    def canonical(edge_modes):
        return jnp.where(flipped, flip_edge(edge_modes), edge_modes)

    out_right = canonical(right_modes[:, :, :, -1])
    out_left = canonical(left_modes[:, :, :, 0])
    from_left = canonical(from_behind(out_right, "elem", 1))
    from_right = canonical(from_behind(out_left, "elem", -1))
    left_next = jnp.concatenate([left_modes[:, :, :, 1:], from_right[:, :, :, None]], axis=3)
    right_prev = jnp.concatenate([from_left[:, :, :, None], right_modes[:, :, :, :-1]], axis=3)
    modal_grid = jnp.concatenate(
        [
            (left_modes + right_prev)[:, :, None],
            (right_modes + left_next)[:, :, None],
            modal_grid[:, :, 2:],
        ],
        axis=2,
    )
    bottom = modal_grid[:, :, :, 0]
    top = modal_grid[:, :, :, 1]
    no_row = jnp.zeros_like(bottom[..., :1])
    new_bottom = bottom + jnp.concatenate([no_row, top[..., :-1]], axis=-1)
    new_top = top + jnp.concatenate([bottom[..., 1:], no_row], axis=-1)
    modal_grid = jnp.concatenate(
        [new_bottom[:, :, :, None], new_top[:, :, :, None], modal_grid[:, :, :, 2:]], axis=3
    )
    return modal_grid.reshape(weak_rhs.shape)


MODES = (P_SIZE + 1) * (P_SIZE + 1)
POINTS = Q * Q
FINE = 3 * NZ // 2
WIDE = 256
LANES = 128
CHUNKS = 4
TABLES = 9
MESH = pl.DeviceIdType.MESH


def halves(table):
    high = table.astype(np.float32).astype(jnp.bfloat16)
    low = (table - high.astype(np.float64)).astype(jnp.bfloat16)
    return high, low


def kernel_tables():
    value, xi, eta, weights, tail, svv, inverse, forward = spectral_tables(P_SIZE, Q, NZ)
    to_point = np.zeros((WIDE, 9 * LANES))
    to_mode = np.zeros((3 * LANES, WIDE))
    for field in range(3):
        rows = slice(field * MODES, (field + 1) * MODES)
        for kind, table in enumerate((value, xi, eta)):
            start = (kind * 3 + field) * LANES
            to_point[rows, start : start + POINTS] = table.T
        to_mode[field * LANES : field * LANES + POINTS, rows] = value
    slope = np.zeros((FINE, NZ))
    for m in range(1, NZ // 2):
        slope[:, 2 * m + 1] = spanwise_scale * m * inverse[:, 2 * m]
        slope[:, 2 * m] = -spanwise_scale * m * inverse[:, 2 * m + 1]

    def triple(table):
        high, low = halves(table)
        return np.concatenate([high, low, high], axis=1)

    lanes = np.zeros((8, WIDE), np.float32)
    lanes[0, : 3 * MODES] = np.tile(tail, 3)
    lanes[1, :MODES] = svv
    lanes[2, :POINTS] = weights
    mode = np.arange(3 * MODES)
    lanes[3, : 3 * MODES] = mode % MODES // (P_SIZE + 1) == 0
    lanes[4, : 3 * MODES] = mode % MODES // (P_SIZE + 1) == 1
    lanes[5, : 3 * MODES] = mode % (P_SIZE + 1) == 0
    lanes[6, : 3 * MODES] = mode % (P_SIZE + 1) == 1
    edges = np.zeros((2, 2, 4, WIDE, LANES), np.float32)
    side = P_SIZE + 1
    for end in range(2):
        for slot in range(4):
            for field in range(3):
                for r in range(side):
                    source = field * MODES + end * side
                    edges[end, 0, slot, source + r, slot * 32 + field * side + r] = 1.0
                    swapped = 1 - r if r < 2 else r
                    sign = 1.0 if r < 2 or r % 2 == 0 else -1.0
                    edges[end, 1, slot, source + swapped, (3 - slot) * 32 + field * side + r] = sign
    edges = edges.reshape(4, 4 * WIDE, LANES).astype(jnp.bfloat16)
    return (
        lanes,
        *halves(to_point),
        triple(inverse),
        triple(slope),
        triple(forward),
        *halves(to_mode),
        edges,
    )


def split(x):
    high = x.astype(jnp.bfloat16)
    return high, (x - high.astype(jnp.float32)).astype(jnp.bfloat16)


def dot(a, b):
    return lax.dot_general(a, b, (((1,), (0,)), ((), ())), preferred_element_type=jnp.float32)


def dot_t(a, b):
    return lax.dot_general(a, b, (((1,), (1,)), ((), ())), preferred_element_type=jnp.float32)


def dot3(x, high, low):
    x_high, x_low = split(x)
    return dot(x_high, high) + dot(x_high, low) + dot(x_low, high)


def stacked_halves(x):
    high, low = split(x)
    return jnp.concatenate([high, high, low], axis=0)


def advance(n_plane, n_elem, flip_ref, *refs):
    n_in = 3 + TABLES
    sources, (joined_ref, sense_ref), held = refs[:n_in], refs[n_in : n_in + 2], refs[n_in + 2 : 2 * n_in + 2]
    fetches = [
        pltpu.make_async_copy(source, target, refs[-1].at[i])
        for i, (source, target) in enumerate(zip(sources, held))
    ]
    for fetch in fetches:
        fetch.start()
    advance_block(n_plane, n_elem, fetches, flip_ref, *held, joined_ref, sense_ref, *refs[2 * n_in + 2 : -1])


def advance_block(n_plane, n_elem, fetches, flip_ref, vel_ref, geo_ref, jac_ref, lane_ref, ph_ref,
            pl_ref, inv_ref, slo_ref, fwd_ref, mh_ref, ml_ref, edge_ref, joined_ref, sense_ref,
            vel_s, pack_s, got_s, weight_s, energy_s, strength_s, point_s, hat_s, back_s, weak_s,
            edge_out, edge_in,
            send_a, recv_a, send_s, recv_s, send_b, recv_b, send_e, recv_e):
    block = lax.axis_index("elem")
    me = lax.axis_index("plane")
    planes = NZ // n_plane
    rows = EY
    columns = n_plane
    elements = rows * columns
    part = rows // CHUNKS
    offsets = [2, 1, 3]
    has_prev = block > 0
    has_next = block < n_elem - 1

    def peer(offset):
        return lax.rem(me + offset, n_plane)

    barrier = pltpu.get_barrier_semaphore()
    for offset in offsets:
        pl.semaphore_signal(barrier, inc=1, device_id=(block, peer(offset)), device_id_type=MESH)

    @pl.when(has_prev)
    def _():
        pl.semaphore_signal(barrier, inc=1, device_id=(block - 1, me), device_id_type=MESH)

    @pl.when(has_next)
    def _():
        pl.semaphore_signal(barrier, inc=1, device_id=(block + 1, me), device_id_type=MESH)

    fetches[0].wait()
    for field in range(3):
        vel_s[field * planes * elements : (field + 1) * planes * elements, 0:MODES] = vel_ref[field]

    lane = lax.broadcasted_iota(jnp.int32, (planes, LANES), 1)
    first_cut = LANES - MODES

    def pack(target, element):
        base = target * rows + element
        u, v, w = [
            vel_s[pl.ds(field * planes * elements + base, planes, stride=elements), :]
            for field in range(3)
        ]
        v_turned = pltpu.roll(v, MODES, 1)
        w_turned = pltpu.roll(w, 2 * MODES - LANES, 1)
        left = jnp.where(lane < MODES, u, v_turned)
        right = jnp.where(
            lane < 2 * MODES - LANES, v_turned, jnp.where(lane < 3 * MODES - LANES, w_turned, 0.0)
        )
        return jnp.concatenate([left, right], axis=1)

    def forward_copy(i, chunk):
        span = pl.ds(chunk * part, part)
        return pltpu.make_async_remote_copy(
            src_ref=pack_s.at[i, span],
            dst_ref=got_s.at[me, span],
            send_sem=send_a.at[i, chunk],
            recv_sem=recv_a.at[i, chunk],
            device_id=(block, peer(offsets[i])),
            device_id_type=MESH,
        )

    def back_copy(i, chunk):
        span = pl.ds(chunk * part, part)
        return pltpu.make_async_remote_copy(
            src_ref=back_s.at[peer(offsets[i]), span],
            dst_ref=weak_s.at[me, span],
            send_sem=send_b.at[i, chunk],
            recv_sem=recv_b.at[i, chunk],
            device_id=(block, peer(offsets[i])),
            device_id_type=MESH,
        )

    def strength_copy(i):
        return pltpu.make_async_remote_copy(
            src_ref=strength_s.at[n_plane],
            dst_ref=strength_s.at[me],
            send_sem=send_s.at[i],
            recv_sem=recv_s.at[i],
            device_id=(block, peer(offsets[i])),
            device_id_type=MESH,
        )

    def edge_copy(i, target):
        return pltpu.make_async_remote_copy(
            src_ref=edge_out.at[i],
            dst_ref=edge_in.at[i],
            send_sem=send_e.at[i],
            recv_sem=recv_e.at[i],
            device_id=(target, me),
            device_id_type=MESH,
        )

    pl.semaphore_wait(
        barrier, len(offsets) + has_prev.astype(jnp.int32) + has_next.astype(jnp.int32)
    )

    def send_chunk(chunk, carry):
        for i, offset in enumerate(offsets):
            for local in range(part):
                pack_s[i, chunk * part + local] = pack(peer(offset), chunk * part + local)
            forward_copy(i, chunk).start()
        return carry

    lax.fori_loop(0, CHUNKS, send_chunk, 0)

    def keep_own(element, carry):
        got_s[me, element] = pack(me, element)
        return carry

    lax.fori_loop(0, rows, keep_own, 0)
    for fetch in fetches[1:-1]:
        fetch.wait()
    start = pl.multiple_of(me * rows, 8)
    area = jac_ref[pl.ds(start, rows), :] * lane_ref[2:3, 0:POINTS]
    weight_s[...] = jnp.zeros_like(weight_s)
    for i in range(4):
        weight_s[i, :, 0:POINTS] = geo_ref[i, pl.ds(start, rows), :] * area
    weight_s[4, :, 0:POINTS] = area

    def work(chunk, carry):
        for i in range(len(offsets)):
            forward_copy(i, chunk).wait_recv()
        x = jnp.concatenate(
            [got_s[source, chunk * part + local] for local in range(part)
             for source in range(n_plane)], axis=0)
        energy_s[chunk] = jnp.sum((x * x).reshape(part, NZ, WIDE), axis=1)
        point_s[...] = dot3(x, ph_ref[...], pl_ref[...])
        for local in range(part):
            element = chunk * part + local
            here = slice(local * NZ, (local + 1) * NZ)
            u = point_s[here, 0:LANES]
            v = point_s[here, LANES : 2 * LANES]
            w = point_s[here, 2 * LANES : 3 * LANES]
            g = [weight_s[i, pl.ds(element, 1), :] for i in range(5)]
            carriers = jnp.concatenate([g[0] * u + g[2] * v, g[1] * u + g[3] * v, g[4] * w], axis=1)
            speeds = dot(inv_ref[...], stacked_halves(carriers))
            slopes = dot(inv_ref[...], stacked_halves(point_s[here, 3 * LANES :]))
            along_z = dot(slo_ref[...], stacked_halves(point_s[here, 0 : 3 * LANES]))
            product = jnp.concatenate(
                [
                    speeds[:, 0:LANES] * slopes[:, f * LANES : (f + 1) * LANES]
                    + speeds[:, LANES : 2 * LANES] * slopes[:, (3 + f) * LANES : (4 + f) * LANES]
                    + speeds[:, 2 * LANES :] * along_z[:, f * LANES : (f + 1) * LANES]
                    for f in range(3)
                ],
                axis=1,
            )
            hat_s[here, :] = dot(fwd_ref[...], stacked_halves(product))
        weak = dot3(hat_s[...], mh_ref[...], ml_ref[...])
        for local in range(part):
            for k in range(n_plane):
                first = local * NZ + k * planes
                back_s[k, chunk * part + local] = weak[first : first + planes]
        for i in range(len(offsets)):
            back_copy(i, chunk).start()
        for local in range(part):
            weak_s[me, chunk * part + local] = back_s[me, chunk * part + local]
        return carry

    lax.fori_loop(0, CHUNKS, work, 0)
    squares = jnp.concatenate([energy_s[c] for c in range(CHUNKS)], axis=0)
    tail_energy = jnp.sum(squares * lane_ref[0:1, :], axis=1, keepdims=True)
    all_energy = jnp.sum(squares, axis=1, keepdims=True)
    log_share = jnp.log((tail_energy + energy_floor) / (all_energy + energy_floor))
    ramp = (log_share - sensor_centre) / sensor_width
    strength = svv_peak / (1.0 + jnp.exp(-ramp))
    strength_s[n_plane] = jnp.broadcast_to(strength, (rows, LANES))
    strength_s[me] = jnp.broadcast_to(strength, (rows, LANES))
    for i in range(len(offsets)):
        strength_copy(i).start()


    for i in range(len(offsets)):
        strength_copy(i).wait_recv()
    sense_ref[...] = strength_s[0:n_plane]

    for chunk in range(CHUNKS):
        for i in range(len(offsets)):
            back_copy(i, chunk).wait_recv()

    fetches[-1].wait()
    flipped = flip_ref[0] == 1
    turn = jnp.where(flipped, 1, 0)
    for i, column in ((0, 0), (1, columns - 1)):
        table = edge_ref[2 * i + turn]
        tiles = []
        for half in range(2):
            picked = jnp.concatenate([weak_s[column, 4 * half + s] for s in range(4)], axis=1)
            high, low = split(picked)
            tiles.append(dot(high, table) + dot(low, table))
        edge_out[i, 0] = jnp.where(flipped, tiles[1], tiles[0])
        edge_out[i, 1] = jnp.where(flipped, tiles[0], tiles[1])

    @pl.when(has_prev)
    def _():
        edge_copy(0, block - 1).start()

    @pl.when(has_next)
    def _():
        edge_copy(1, block + 1).start()

    side = P_SIZE + 1
    is_left = lane_ref[3:4, :] > 0.0
    is_right = lane_ref[4:5, :] > 0.0

    def join_row(row, carry):
        strip = [weak_s[column, row] for column in range(columns)]
        for column in range(columns):
            total = strip[column]
            if column > 0:
                total = total + jnp.where(is_left, pltpu.roll(strip[column - 1], WIDE - side, 1), 0.0)
            if column < columns - 1:
                total = total + jnp.where(is_right, pltpu.roll(strip[column + 1], side, 1), 0.0)
            got_s[column, row] = total
        return carry

    lax.fori_loop(0, rows, join_row, 0)

    @pl.when(has_next)
    def _():
        edge_copy(0, block + 1).wait_recv()

    @pl.when(block == n_elem - 1)
    def _():
        edge_in[0] = jnp.zeros((2, planes, LANES), jnp.float32)

    @pl.when(has_prev)
    def _():
        edge_copy(1, block - 1).wait_recv()

    @pl.when(block == 0)
    def _():
        edge_in[1] = jnp.zeros((2, planes, LANES), jnp.float32)

    for i, column in ((1, 0), (0, columns - 1)):
        table = edge_ref[2 * (1 - i) + turn]
        for half in range(2):
            tile = jnp.where(flipped, edge_in[i, 1 - half], edge_in[i, half])
            high, low = split(tile)
            spread = dot_t(high, table) + dot_t(low, table)
            for s in range(4):
                got_s[column, 4 * half + s] += spread[:, s * WIDE : (s + 1) * WIDE]

    joined_ref[...] = got_s[...]

    for i in range(len(offsets)):
        strength_copy(i).wait_send()
        for chunk in range(CHUNKS):
            forward_copy(i, chunk).wait_send()
            back_copy(i, chunk).wait_send()

    @pl.when(has_prev)
    def _():
        edge_copy(0, block - 1).wait_send()

    @pl.when(has_next)
    def _():
        edge_copy(1, block + 1).wait_send()


def finish(joined_ref, sense_ref, vel_ref, lane_ref, adv_ref, svv_ref, out_s):
    planes = joined_ref.shape[2]
    is_bottom = lane_ref[5:6, :] > 0.0
    is_top = lane_ref[6:7, :] > 0.0
    factor = -sense_ref[0] * lane_ref[1:2, 0:LANES]
    svv_ref[...] = vel_ref[...] * factor[:, 0:MODES]
    strip = [joined_ref[0, row] for row in range(EY)]
    for row in range(EY):
        total = strip[row]
        if row > 0:
            total = total + jnp.where(is_bottom, pltpu.roll(strip[row - 1], WIDE - 1, 1), 0.0)
        if row < EY - 1:
            total = total + jnp.where(is_top, pltpu.roll(strip[row + 1], 1, 1), 0.0)
        fields = (
            total[:, 0:LANES],
            pltpu.roll(total, WIDE - MODES, 1)[:, 0:LANES],
            pltpu.roll(total, WIDE - 2 * MODES, 1)[:, 0:LANES],
        )
        for field in range(3):
            out_s[pl.ds(field * planes * EY + row, planes, stride=EY), :] = fields[field]
    for field in range(3):
        block = out_s[field * planes * EY : (field + 1) * planes * EY, 0:MODES]
        adv_ref[field] = block.reshape(planes, EY, MODES)


def kernel_body(n_plane, n_elem, velocity, geometry, jacobian, frame_flip):
    planes, elements = velocity.shape[1], velocity.shape[3]
    tables = [jnp.asarray(table) for table in kernel_tables()]
    vel = velocity.transpose(0, 1, 3, 2).reshape(3, planes * elements, MODES)
    geo = geometry.transpose(0, 2, 1)
    jac = jacobian.transpose(1, 0)
    inputs = [vel, geo, jac, *tables]
    whole = pl.BlockSpec(memory_space=pltpu.VMEM)
    part = EY // CHUNKS
    f32 = jnp.float32
    dma = pltpu.SemaphoreType.DMA
    others = n_plane - 1
    joined, sense = pl.pallas_call(
        functools.partial(advance, n_plane, n_elem),
        out_shape=(
            jax.ShapeDtypeStruct((n_plane, EY, planes, WIDE), f32),
            jax.ShapeDtypeStruct((n_plane, EY, LANES), f32),
        ),
        in_specs=[pl.BlockSpec(memory_space=pltpu.SMEM)] + [pl.BlockSpec(memory_space=pltpu.HBM)] * len(inputs),
        out_specs=(whole, whole),
        scratch_shapes=[pltpu.VMEM(x.shape, x.dtype) for x in inputs]
        + [
            pltpu.VMEM((3 * planes * elements, LANES), f32),
            pltpu.VMEM((others, EY, planes, WIDE), f32),
            pltpu.VMEM((n_plane, EY, planes, WIDE), f32),
            pltpu.VMEM((5, EY, LANES), f32),
            pltpu.VMEM((CHUNKS, part, WIDE), f32),
            pltpu.VMEM((n_plane + 1, EY, LANES), f32),
            pltpu.VMEM((part * NZ, 9 * LANES), f32),
            pltpu.VMEM((part * NZ, 3 * LANES), f32),
            pltpu.VMEM((n_plane, EY, planes, WIDE), f32),
            pltpu.VMEM((n_plane, EY, planes, WIDE), f32),
            pltpu.VMEM((2, 2, planes, LANES), f32),
            pltpu.VMEM((2, 2, planes, LANES), f32),
            dma((others, CHUNKS)),
            dma((others, CHUNKS)),
            dma((others,)),
            dma((others,)),
            dma((others, CHUNKS)),
            dma((others, CHUNKS)),
            dma((2,)),
            dma((2,)),
            dma((len(inputs),)),
        ],
        compiler_params=pltpu.CompilerParams(
            collective_id=0, has_side_effects=True, vmem_limit_bytes=61 * 1024 * 1024
        ),
    )(frame_flip, *inputs)

    slab = pl.BlockSpec((3, planes, EY, MODES), lambda c: (0, 0, c, 0))
    full = jax.ShapeDtypeStruct((3, planes, elements, MODES), f32)
    advection, svv = pl.pallas_call(
        finish,
        out_shape=(full, full),
        grid=(n_plane,),
        in_specs=[
            pl.BlockSpec((1, EY, planes, WIDE), lambda c: (c, 0, 0, 0)),
            pl.BlockSpec((1, EY, LANES), lambda c: (c, 0, 0)),
            slab,
            pl.BlockSpec((8, WIDE), lambda c: (0, 0)),
        ],
        out_specs=(slab, slab),
        scratch_shapes=[pltpu.VMEM((3 * planes * EY, LANES), f32)],
        compiler_params=pltpu.CompilerParams(vmem_limit_bytes=61 * 1024 * 1024),
    )(joined, sense, velocity.transpose(0, 1, 3, 2), tables[0])
    return advection.transpose(0, 1, 3, 2), svv.transpose(0, 1, 3, 2)


def body(velocity, geometry, jacobian, frame_flip):
    value_table, xi_table, eta_table, point_weights, tail_mask, svv_weight, inverse, forward = (
        jnp.asarray(table.astype(np.float32)) for table in spectral_tables(P_SIZE, Q, NZ)
    )
    planes_here = velocity.shape[1]
    position = lax.axis_index("plane")
    wavenumbers = (position * (planes_here // 2) + jnp.arange(planes_here // 2)).astype(jnp.float32)
    zcoeffs = z_slope(velocity, wavenumbers)
    stacked = point_values(velocity, zcoeffs, geometry, value_table, xi_table, eta_table)
    gathered = to_points(stacked)
    nonlinear = advect(gathered, inverse, forward)
    returned = to_planes(nonlinear)
    weak_rhs = project(returned, jacobian, value_table, point_weights)
    tail_part, all_part = energies(velocity, tail_mask)
    tail_energy, all_energy = lax.psum((tail_part, all_part), "plane")
    strength = strength_ramp(tail_energy, all_energy)
    svv_force = -strength[None, None, None, :] * svv_weight[None, None, :, None] * velocity
    advection = assemble(weak_rhs, frame_flip[0])
    return (advection, svv_force)


def solution(mesh):
    n_plane, n_elem = mesh.shape["plane"], mesh.shape["elem"]
    fits = n_plane == 4 and (NZ // n_plane) % 16 == 0
    return jax.shard_map(
        functools.partial(kernel_body, n_plane, n_elem) if fits else body,
        mesh=mesh,
        in_specs=(
            P(None, "plane", None, "elem"),
            P(None, None, "elem"),
            P(None, "elem"),
            P("elem"),
        ),
        out_specs=(P(None, "plane", None, "elem"), P(None, "plane", None, "elem")),
        check_vma=False,
    )
```
